512 devices in a mesh: expert: 64 (over z, y_hi, x), tensor: 8 (over y_lo, core).
Axes of the slice: x: 4, y: 8 (y_hi: 2, y_lo: 4; y = y_hi * 4 + y_lo), z: 8, core: 2. Of those that a mesh axis runs over, the one named last changes fastest.
Arguments:
- grad_out: bfloat16 [8192, 4096], P('expert', 'tensor'), may hold values from -6 to 6
- dense_gate: bfloat16 [8192, 3072], P('expert', 'tensor'), may hold values from -6 to 6
- dense_up: bfloat16 [8192, 3072], P('expert', 'tensor'), may hold values from -6 to 6
- w_gate: bfloat16 [4096, 3072], P('expert', 'tensor'), may hold values from -0.109375 to 0.109375
- w_up: bfloat16 [4096, 3072], P('expert', 'tensor'), may hold values from -0.109375 to 0.109375
- w_down: bfloat16 [3072, 4096], P('tensor', 'expert'), may hold values from -0.09375 to 0.09375
- routes: int32 [8192, 2], P('expert'), may hold values from 0 to 63, all different within a row; in each aligned block of 128 rows (0 to 127, 128 to 255, ...) at most 5 rows name the same one
- route_weight: bfloat16 [8192, 2], P('expert'), may hold values from 0.25 to 1
- expert_down: bfloat16 [64, 3072, 4096], P('expert', 'tensor'), may hold values from -0.09375 to 0.09375
- expert_hidden: bfloat16 [64, 320, 3072], P('expert', None, 'tensor'), may hold values from -0.107910156 to 0.107910156
Outputs:
- input_grad: bfloat16 [8192, 4096], P('expert', 'tensor')
- hidden_grad: bfloat16 [64, 320, 3072], P('expert', None, 'tensor')
- route_grad: float32 [8192, 2], P('expert')
The draws below stay inside these ranges and needn't reach their ends.
Inputs may be any that keep to these rules, and one draw needn't show every extreme that they name: `routes`: the two experts of a row differ. Among the rows of one index of expert (aligned blocks of 128 rows) no expert is named more than 5 times, a bound that some block reaches.
All inputs are finite; a program needn't handle non-finite values.
Results may differ from the reference program's by a relative error of at most 0.0049.
Values may be sent and summed in bfloat16 or wider, within the bound.
A program may use at most 64 MiB of HBM per device.

```python
import math
import jax
import jax.numpy as jnp
import numpy as np
from jax import lax

D = 4096
FF = 3072
H = 3072
TOP = 2
TOK_DEV = 128
EXPERTS = 64
CAP = 5
SLOTS = 320
TOKENS = 8192
N_EXPERT = 64


def shard_levels(stream_key, dims, pieces, smallest, largest):
    level, own = 1.0, jax.random.fold_in(stream_key, 6)
    for axis_at, shards_of in pieces:
        heights = jnp.exp(jax.random.uniform(jax.random.fold_in(own, axis_at), (shards_of,), jnp.float32, smallest / len(pieces), largest / len(pieces)))
        level = level * jnp.repeat(heights, dims[axis_at] // shards_of).reshape([-1 if axis == axis_at else 1 for axis in range(len(dims))])
    return level


def shared_out(rng, own, number, rows, number_of, top, most, slope):
    sequence = jax.random.permutation(rng, number_of)
    packed, common = shares(number_of, rows * top, most, slope, True), shares(number_of, rows * top, most, slope, False)
    places = jnp.arange(number_of)

    def named(tallies, offset_by):
        used = int((tallies > 0).sum())
        fixed = max(1, used // 4)
        passed = fixed + (places - fixed + offset_by * (used - fixed)) % max(1, number_of - fixed)
        return jnp.zeros((number_of,), jnp.int32).at[sequence[jnp.where(places < fixed, places, passed)]].set(jnp.asarray(tallies, jnp.int32))

    tallies = jnp.where(number % 4 == 0, named(packed, number // 4), named(common, number - number // 4 - 1))
    mixed = jax.random.permutation(jax.random.fold_in(own, 3), number_of)
    donor, sink = mixed[0:number_of // 2 * 2:2], mixed[1:number_of // 2 * 2:2]
    slack = jnp.minimum(tallies[donor] - 1, most - tallies[sink]) // 2
    slack = jnp.where((donor == sequence[0]) | (sink == sequence[0]) | (tallies[sink] == 0), 0, jnp.maximum(slack, 0))
    passed = jax.random.randint(jax.random.fold_in(own, 4), (number_of // 2,), 0, 1 << 20) % (slack + 1)
    tallies = tallies.at[donor].add(-passed).at[sink].add(passed)
    labels = jnp.searchsorted(jnp.cumsum(tallies), jnp.arange(rows * top), side="right").astype(jnp.int32)
    table = labels.reshape(top, rows).T
    table = table[jax.random.permutation(jax.random.fold_in(own, 1), rows)]
    offset_by = jax.random.randint(jax.random.fold_in(own, 2), (rows, 1), 0, top)
    return jnp.take_along_axis(table, (jnp.arange(top)[None, :] + offset_by) % top, axis=1)


def shares(count, total, bound, skew, full):
    loads = [(1 << 20) // math.isqrt(rank ** skew) + 1 for rank in range(1, count + 1)]
    largest = bound if full else min(bound, max(-(-total // count), total * loads[0] // sum(loads)))
    least = 1 if total - largest >= count - 1 else 0
    counts, rest = [largest] + [least] * (count - 1), total - largest - least * (count - 1)
    while rest > 0:
        movable = [i for i in range(1, count) if counts[i] < largest] or [i for i in range(1, count) if counts[i] < bound]
        pool, budget = sum([loads[i] for i in movable]), rest
        for i in movable:
            extra = min(bound - counts[i], max(1, budget * loads[i] // pool), rest)
            counts[i] = counts[i] + extra
            rest = rest - extra
    return np.array(counts)


def scatter_about(stream_key, dims, deviation, most, pieces=(), held_as=jnp.bfloat16):
    factor_of = shard_levels(stream_key, dims, pieces, -0.22, 0.18) if pieces else 1.0
    array = jax.random.normal(stream_key, dims, jnp.float32) * deviation * factor_of
    return jnp.minimum(jnp.maximum(array, -most), most).astype(held_as)


def setup_inputs(seed: int = 0) -> dict:
    seeds = jax.random.split(jax.random.key(seed), 11)
    grad_out = scatter_about(seeds[0], (TOKENS, D), 1.0, 6.0, ((0, 64), (1, 8)))
    dense_gate = scatter_about(seeds[1], (TOKENS, FF), 1.0, 6.0, ((0, 64), (1, 8)))
    dense_up = scatter_about(seeds[2], (TOKENS, FF), 1.0, 6.0, ((0, 64), (1, 8)))
    w_gate = scatter_about(seeds[3], (D, FF), FF ** -0.5, 0.109375, ((0, 64), (1, 8)))
    w_up = scatter_about(seeds[4], (D, FF), FF ** -0.5, 0.109375, ((0, 64), (1, 8)))
    w_down = scatter_about(seeds[5], (FF, D), D ** -0.5, 0.09375, ((0, 8), (1, 64)))
    routes_keys = jax.random.split(jax.random.fold_in(seeds[6], 1), TOKENS // TOK_DEV)
    routes_turns = jax.random.permutation(jax.random.fold_in(seeds[6], 3), TOKENS // TOK_DEV)
    routes = jax.vmap(lambda own, number: shared_out(jax.random.fold_in(seeds[6], 2), own, number, TOK_DEV, EXPERTS, TOP, CAP, 2))(routes_keys, routes_turns).reshape((TOKENS, TOP))
    route_weight = jnp.clip(0.25 + 0.75 * jax.random.uniform(seeds[7], (TOKENS, TOP), jnp.float32) ** shard_levels(seeds[7], (TOKENS, TOP), ((0, 64),), -0.2, 0.2), 0.25, 1.0).astype(jnp.bfloat16)
    expert_down = scatter_about(seeds[8], (EXPERTS, H, D), D ** -0.5, 0.09375, ((0, 64), (1, 8)))
    expert_hidden = scatter_about(seeds[9], (EXPERTS, SLOTS, H), (H ** -0.5), 0.107910156, ((0, 64), (2, 8)))
    return dict(grad_out=grad_out, dense_gate=dense_gate, dense_up=dense_up, w_gate=w_gate, w_up=w_up, w_down=w_down, routes=routes, route_weight=route_weight, expert_down=expert_down, expert_hidden=expert_hidden)


def reference(grad_out, dense_gate, dense_up, w_gate, w_up, w_down, routes, route_weight, expert_down, expert_hidden):
    def dense_block(args):
        grad_rows, gate_rows, up_rows = args
        hidden_delta = jnp.dot(grad_rows, w_down.T, preferred_element_type=jnp.float32)
        gate_f = gate_rows.astype(jnp.float32)
        up_f = up_rows.astype(jnp.float32)
        sigmoid_gate = jax.nn.sigmoid(gate_f)
        swish_gate = gate_f * sigmoid_gate
        slope_gate = sigmoid_gate * (1.0 + gate_f * (1.0 - sigmoid_gate))
        gate_delta = (hidden_delta * up_f * slope_gate).astype(jnp.bfloat16)
        up_delta = (hidden_delta * swish_gate).astype(jnp.bfloat16)
        summed = jnp.dot(gate_delta, w_gate.T, preferred_element_type=jnp.float32) + jnp.dot(up_delta, w_up.T, preferred_element_type=jnp.float32)
        return summed.astype(jnp.bfloat16)

    input_grad = lax.map(dense_block, (grad_out.reshape(N_EXPERT, TOK_DEV, D), dense_gate.reshape(N_EXPERT, TOK_DEV, FF), dense_up.reshape(N_EXPERT, TOK_DEV, FF))).reshape(TOKENS, D)

    grouped = routes.reshape(N_EXPERT, TOK_DEV * TOP)
    onehot = (grouped[:, :, None] == jnp.arange(EXPERTS, dtype=jnp.int32)[None, None, :]).astype(jnp.int32)
    earlier = jnp.cumsum(onehot, axis=1) - onehot
    slot_rank = jnp.sum(earlier * onehot, axis=2)
    position = (jnp.arange(N_EXPERT, dtype=jnp.int32)[:, None] * CAP + slot_rank).reshape(-1).astype(jnp.int32)
    expert_ids = routes.reshape(-1).astype(jnp.int32)
    token_ids = (jnp.arange(TOKENS * TOP, dtype=jnp.int32) // TOP).astype(jnp.int32)
    token_table = jnp.zeros((EXPERTS, SLOTS), jnp.int32).at[expert_ids, position].set(token_ids)
    live_table = jnp.zeros((EXPERTS, SLOTS), jnp.int32).at[expert_ids, position].set(1)
    weight_table = jnp.zeros((EXPERTS, SLOTS), jnp.float32).at[expert_ids, position].set(route_weight.reshape(-1).astype(jnp.float32))

    def expert_block(args):
        weights, tokens_here, live, scale, saved = args
        rows = jnp.where(live[:, None] > 0, grad_out[tokens_here], jnp.zeros((), grad_out.dtype))
        slot_delta = jnp.dot(rows, weights.T, preferred_element_type=jnp.float32)
        scaled = (scale[:, None] * slot_delta).astype(jnp.bfloat16)
        return scaled, jnp.sum(saved.astype(jnp.float32) * slot_delta, axis=1)

    hidden_grad, partial_value = lax.map(expert_block, (expert_down, token_table, live_table, weight_table, expert_hidden))
    route_grad = partial_value[expert_ids, position].reshape(TOKENS, TOP)
    return input_grad, hidden_grad, route_grad
```

```python
import jax
import jax.numpy as jnp
import numpy as np
from jax import lax
from jax.experimental import pallas as pl
from jax.experimental.pallas import tpu as pltpu
from jax.sharding import PartitionSpec as P

MESH = pl.DeviceIdType.MESH
F32 = jnp.float32
BF16 = jnp.bfloat16
CAP = 5
BLK = 48
N_COPY = 160


def dot_nt(a, b):
    return lax.dot_general(a, b, (((1,), (1,)), ((), ())), preferred_element_type=F32)


def dot_tn(a, b):
    return lax.dot_general(a, b, (((0,), (0,)), ((), ())), preferred_element_type=F32)


def dot_nn(a, b):
    return jnp.dot(a, b, preferred_element_type=F32)


def tables():
    p2 = np.zeros((8 * BLK, 8 * BLK), np.float32)
    p3 = np.zeros((320, 8 * BLK), np.float32)
    p4 = np.zeros((320, 8 * BLK), np.float32)
    m5 = np.zeros((320, 128), np.float32)
    for j in range(8):
        for z in range(8):
            p2[j * BLK + 40 + z, z * BLK + 40 + j] = 1
            for s in range(CAP):
                p2[j * BLK + z * CAP + s, z * BLK + j * CAP + s] = 1
                row = z * 40 + j * CAP + s
                p3[row, j * BLK + z * CAP + s] = 1
                p4[row, j * BLK + 40 + z] = 1
                m5[row, s] = 1
    return p2, p3, p4, m5


def kernel(
    grad, gate, up, wd, wg, wu, routes, rw, ed_hbm, hid, p2, p3, p4, m5,
    out_g, out_h, out_r,
    W, G, SL, S1, R1, S2, R2, ED, acc, K, XS, XR, YS, YR, RT0, RT1, ST2, RT2,
    ssem, rsem, lsem, ysend, yrecv,
):
    e = lax.axis_index("expert")
    t = lax.axis_index("tensor")
    z = e // 8
    j = lax.rem(e, 8)
    yh = j // 4
    x = lax.rem(j, 4)
    yl = t // 2
    c = lax.rem(t, 2)
    yo = 1 - yh

    def zz(d):
        return lax.rem(z + d + 8, 8)

    def xx(d):
        return lax.rem(x + d, 4)

    def z_dev(d):
        return (zz(d) * 8 + j, t)

    def x_dev(d):
        return (z * 8 + yh * 4 + xx(d), t)

    def j_dev(d):
        return (z * 8 + lax.rem(j + d, 8), t)

    y_dev = (z * 8 + yo * 4 + x, t)
    sibling = (e, yl * 2 + 1 - c)

    def yl_dev(d):
        return (e, lax.rem(yl + d, 4) * 2 + c)

    def t_dev(d):
        return (e, lax.rem(t + d, 8))

    barrier = pltpu.get_barrier_semaphore()
    for d in range(1, 8):
        for dev in (z_dev(d), j_dev(d), t_dev(d)):
            pl.semaphore_signal(barrier, inc=1, device_id=dev, device_id_type=MESH)

    ed_copy = pltpu.make_async_copy(ed_hbm, ED, lsem)
    ed_copy.start()

    count = [0]
    sends = []

    def send(src, dst, dev):
        i = count[0]
        count[0] += 1
        copy = pltpu.make_async_remote_copy(
            src_ref=src, dst_ref=dst, send_sem=ssem.at[i], recv_sem=rsem.at[i],
            device_id=dev, device_id_type=MESH,
        )
        copy.start()
        sends.append(copy)
        return copy

    W[0, z, yh, x] = wd[...]
    W[1, z, yh, x] = wg[...]
    W[2, z, yh, x] = wu[...]
    G[t] = grad[...]

    lane = lax.broadcasted_iota(jnp.int32, (128, 128), 1).astype(F32)
    row = lax.broadcasted_iota(jnp.int32, (128, 128), 0).astype(F32)
    lane_b = lax.broadcasted_iota(jnp.int32, (128, 8 * BLK), 1).astype(F32)
    route = [routes[:, k : k + 1] for k in range(2)]
    onehot = [(route[k].astype(F32) == lane).astype(F32) for k in range(2)]
    lower = (lane < row).astype(BF16)
    earlier = dot_nn(lower, (onehot[0] + onehot[1]).astype(BF16))
    rank = [
        jnp.sum(earlier * onehot[0], axis=1, keepdims=True),
        jnp.sum((earlier + onehot[0]) * onehot[1], axis=1, keepdims=True),
    ]
    slot_map = jnp.zeros((128, 8 * BLK), F32)
    weight_rows = jnp.zeros((8 * BLK, 128), F32)
    for k in range(2):
        base = (lax.shift_right_logical(route[k], 3) * BLK).astype(F32)
        low = lax.bitwise_and(route[k], 7).astype(F32)
        slot_map += (base + low * CAP + rank[k] == lane_b).astype(F32)
        spare = (base + low + 40.0 == lane_b).astype(BF16)
        value = jnp.where(lane == rank[k], rw[:, k : k + 1].astype(F32), 0.0).astype(BF16)
        weight_rows += dot_tn(spare, value)
    filled = dot_tn(slot_map.astype(BF16), grad[...])
    first = (filled[:, 0:128] + weight_rows).astype(BF16)
    for k in range(8):
        S1[k, :, 0:128] = first[k * BLK : (k + 1) * BLK]
        S1[k, :, 128:512] = filled[k * BLK : (k + 1) * BLK, 128:512].astype(BF16)
    R1[z] = S1[z]

    pl.semaphore_wait(barrier, 21)

    disp1 = [send(S1.at[zz(d)], R1.at[z], z_dev(d)) for d in range(1, 8)]

    kinds = (pl.ds(0, 1), pl.ds(1, 2))

    def a_ring(kd, step, right):
        sign = 1 if right else -1
        zc = zz(-sign * (step - 1))
        ref = W.at[kinds[kd], zc, yh, x]
        if step == 4:
            ref = W.at[kinds[kd], zc, yh, x, pl.ds(0 if right else 32, 32)]
        return send(ref, ref, z_dev(sign))

    def b_ring(kd, step, right):
        sign = 1 if right else -1
        zc = zz(-sign * (step - 1))
        ref = W.at[kinds[kd], zc, yo]
        if step == 4:
            ref = W.at[kinds[kd], zc, yo, pl.ds(0 if right else 2, 2)]
        return send(ref, ref, z_dev(sign))

    def x_send(kd, delta, half):
        ref = W.at[kinds[kd], zz(delta), half, x]
        return [send(ref, ref, x_dev(d)) for d in range(1, 4)]

    def gather_start(buf):
        own = buf.at[t]
        return [send(own, own, yl_dev(d)) for d in range(1, 4)] + [send(own, own, sibling)]

    def gather_forward(buf, first_copies):
        out = []
        for d in range(1, 4):
            first_copies[d - 1].wait_recv()
            ref = buf.at[lax.rem(yl - d + 4, 4) * 2 + c]
            out.append(send(ref, ref, sibling))
        return out

    a = {}
    b = {}
    ax = {}
    for kd in range(2):
        ref = W.at[kinds[kd], z, yh, x]
        for right in (True, False):
            a[kd, 1, right] = a_ring(kd, 1, right)
        a[kd, 0] = send(ref, ref, y_dev)
        if kd == 0:
            tok = gather_start(G)
        ax[kd, 0] = x_send(kd, 0, yh)

    def a_step(kd, step):
        a[kd, step, True].wait_recv()
        if step < 4:
            a[kd, step + 1, True] = a_ring(kd, step + 1, True)
        a[kd, step, False].wait_recv()
        if step < 4:
            a[kd, step + 1, False] = a_ring(kd, step + 1, False)
            ax[kd, -step] = x_send(kd, -step, yh)
            ax[kd, step] = x_send(kd, step, yh)
        else:
            ax[kd, 4] = x_send(kd, 4, yh)

    def b_step(kd, step):
        b[kd, step, True].wait_recv()
        if step < 4:
            b[kd, step + 1, True] = b_ring(kd, step + 1, True)
        b[kd, step, False].wait_recv()
        if step < 4:
            b[kd, step + 1, False] = b_ring(kd, step + 1, False)

    bx = {}

    def b_open(kd):
        for copy in bx[kd]:
            copy.wait_recv()
        for right in (True, False):
            b[kd, 1, right] = b_ring(kd, 1, right)

    a_step(0, 1)
    a[0, 0].wait_recv()
    bx[0] = x_send(0, 0, yo)
    for copy in disp1:
        copy.wait_recv()
    shuffled = dot_nn(p2[...], R1[...].reshape(8 * BLK, 512)).astype(BF16)
    S2[...] = shuffled.reshape(8, BLK, 512)
    R2[j] = S2[j]
    disp2 = [send(S2.at[lax.rem(j + d, 8)], R2.at[j], j_dev(d)) for d in range(1, 8)]

    a_step(1, 1)
    a[1, 0].wait_recv()
    bx[1] = x_send(1, 0, yo)
    tok_fwd = gather_forward(G, tok)
    a_step(0, 2)
    b_open(0)
    a_step(1, 2)
    b_open(1)

    for copy in disp2:
        copy.wait_recv()
    arrived = R2[...].reshape(8 * BLK, 512)
    SL[t] = dot_nn(p3[...], arrived).astype(BF16)
    slots = gather_start(SL)
    slot_weight = jnp.sum(dot_nn(p4[...], arrived[:, 0:128]) * m5[...], axis=1, keepdims=True)

    a_step(0, 3)
    b_step(0, 1)
    a_step(1, 3)
    a_step(0, 4)
    b_step(0, 2)
    a_step(1, 4)
    b_step(1, 1)
    b_step(0, 3)
    b_step(0, 4)

    tok[3].wait_recv()
    for copy in tok_fwd:
        copy.wait_recv()
    for delta in (0, -1, 1, -2, 2, -3, 3, 4):
        for copy in ax[0, delta]:
            copy.wait_recv()
    hd = jnp.zeros((128, 384), F32)
    for k in range(8):
        hd += dot_nn(G[k], W[0, k].reshape(512, 384))
    gate_f = gate[...].astype(F32)
    up_f = up[...].astype(F32)
    sig = jax.nn.sigmoid(gate_f)
    swish = gate_f * sig
    slope = sig * (1.0 + gate_f * (1.0 - sig))
    gd = (hd * up_f * slope).astype(BF16)
    ud = (hd * swish).astype(BF16)

    b_step(1, 2)

    slots_fwd = gather_forward(SL, slots)
    ed_copy.wait()

    def expert_term(idx):
        cols = pl.ds(pl.multiple_of(idx * 512, 512), 512)
        return dot_nt(SL[idx], ED[:, cols])

    acc[...] = expert_term(t)
    for d in range(1, 4):
        acc[...] += expert_term(lax.rem(yl - d + 4, 4) * 2 + c)
    slots[3].wait_recv()
    acc[...] += expert_term(yl * 2 + 1 - c)
    for d in range(1, 4):
        slots_fwd[d - 1].wait_recv()
        acc[...] += expert_term(lax.rem(yl - d + 4, 4) * 2 + 1 - c)
    out_h[...] = (slot_weight * acc[...]).astype(BF16)
    part = jnp.sum(hid[...].astype(F32) * acc[...], axis=1, keepdims=True)
    diag = lax.broadcasted_iota(jnp.int32, (40, 128), 0) == lax.broadcasted_iota(
        jnp.int32, (40, 128), 1
    )
    tile = jnp.concatenate(
        [
            jnp.sum(jnp.where(diag, part[k * 40 : (k + 1) * 40], 0.0), axis=0, keepdims=True)
            for k in range(8)
        ],
        axis=0,
    )
    RT0[t] = tile
    own = RT0.at[t]
    ret0 = [send(own, own, t_dev(d)) for d in range(1, 8)]

    b_step(1, 3)

    for copy in ret0:
        copy.wait_recv()
    RT1[j] = jnp.sum(RT0[...], axis=0)
    own1 = RT1.at[j]
    ret1 = [send(own1, own1, j_dev(d)) for d in range(1, 8)]

    def pair(q):
        def block(zb):
            return dot_nt(gd, W[1, zb].reshape(512, 384)) + dot_nt(ud, W[2, zb].reshape(512, 384))

        XS[q] = block(2 * q + 1 - c).astype(BF16)
        copy = send(XS.at[q], XR.at[q], sibling)
        K[q] = block(2 * q + c)
        return copy

    def y_copy(q, src):
        return pltpu.make_async_remote_copy(
            src_ref=YS.at[q], dst_ref=YR.at[src], send_sem=ysend.at[q], recv_sem=yrecv.at[src],
            device_id=(e, q * 2 + c), device_id_type=MESH,
        )

    def pass_on(q, copy):
        copy.wait_recv()
        K[q] = K[q] + XR[q].astype(F32)

        @pl.when(q != yl)
        def _():
            YS[q] = K[q].astype(BF16)
            y_copy(q, yl).start()

    def x_wait(delta):
        for copy in ax[1, delta]:
            copy.wait_recv()

    zq = z // 2

    def qq(d):
        return lax.rem(zq + d, 4)

    for delta in (0, -1, 1):
        x_wait(delta)
    p0 = pair(qq(0))

    for copy in ret1:
        copy.wait_recv()
    for k in range(8):
        ST2[k] = RT1[:, k, :]
    RT2[z] = ST2[z]
    ret2 = [send(ST2.at[zz(d)], RT2.at[z], z_dev(d)) for d in range(1, 8)]

    pass_on(qq(0), p0)
    for delta in (-2, 2, -3, 3):
        x_wait(delta)
    p1 = pair(qq(3))
    p2_ = pair(qq(1))
    pass_on(qq(3), p1)
    pass_on(qq(1), p2_)
    b_step(1, 4)
    x_wait(4)
    p3_ = pair(qq(2))

    for copy in ret2:
        copy.wait_recv()
    back = RT2[...].reshape(64, 128)
    jf = (j * CAP).astype(F32)
    for k in range(2):
        scores = jnp.dot(
            onehot[k][:, 0:64], back, preferred_element_type=F32, precision=lax.Precision.HIGHEST
        )
        out_r[:, k : k + 1] = jnp.sum(
            jnp.where(lane == rank[k] + jf, scores, 0.0), axis=1, keepdims=True
        )

    pass_on(qq(2), p3_)
    total = K[yl]
    for d in range(1, 4):
        src = lax.rem(yl + d, 4)
        y_copy(src, src).wait_recv()
        total += YR[src].astype(F32)
    out_g[...] = total.astype(BF16)
    for d in range(1, 4):
        q = lax.rem(yl + d, 4)
        y_copy(q, q).wait_send()
    for copy in sends:
        copy.wait_send()


def body(
    grad_out, dense_gate, dense_up, w_gate, w_up, w_down, routes, route_weight,
    expert_down, expert_hidden,
):
    p2, p3, p4, m5 = tables()
    vmem = pl.BlockSpec(memory_space=pltpu.VMEM)
    hbm = pl.BlockSpec(memory_space=pl.ANY)
    out_g, out_h, out_r = pl.pallas_call(
        kernel,
        out_shape=(
            jax.ShapeDtypeStruct((128, 512), BF16),
            jax.ShapeDtypeStruct((320, 384), BF16),
            jax.ShapeDtypeStruct((128, 2), F32),
        ),
        in_specs=[vmem] * 8 + [hbm] + [vmem] * 5,
        out_specs=(vmem, vmem, vmem),
        scratch_shapes=[
            pltpu.VMEM((3, 8, 2, 4, 64, 384), BF16),
            pltpu.VMEM((8, 128, 512), BF16),
            pltpu.VMEM((8, 320, 512), BF16),
            pltpu.VMEM((8, BLK, 512), BF16),
            pltpu.VMEM((8, BLK, 512), BF16),
            pltpu.VMEM((8, BLK, 512), BF16),
            pltpu.VMEM((8, BLK, 512), BF16),
            pltpu.VMEM((384, 4096), BF16),
            pltpu.VMEM((320, 384), F32),
            pltpu.VMEM((4, 128, 512), F32),
            pltpu.VMEM((4, 128, 512), BF16),
            pltpu.VMEM((4, 128, 512), BF16),
            pltpu.VMEM((4, 128, 512), BF16),
            pltpu.VMEM((4, 128, 512), BF16),
            pltpu.VMEM((8, 8, 128), F32),
            pltpu.VMEM((8, 8, 128), F32),
            pltpu.VMEM((8, 8, 128), F32),
            pltpu.VMEM((8, 8, 128), F32),
            pltpu.SemaphoreType.DMA((N_COPY,)),
            pltpu.SemaphoreType.DMA((N_COPY,)),
            pltpu.SemaphoreType.DMA,
            pltpu.SemaphoreType.DMA((4,)),
            pltpu.SemaphoreType.DMA((4,)),
        ],
        compiler_params=pltpu.CompilerParams(
            collective_id=0, has_side_effects=True, vmem_limit_bytes=48 << 20
        ),
    )(
        grad_out, dense_gate, dense_up, w_down.T, w_gate, w_up, routes, route_weight,
        expert_down[0], expert_hidden[0],
        jnp.asarray(p2, BF16), jnp.asarray(p3, BF16), jnp.asarray(p4, BF16), jnp.asarray(m5, F32),
    )
    return out_g, out_h[None], out_r


def solution(mesh):
    in_specs = (
        P("expert", "tensor"),
        P("expert", "tensor"),
        P("expert", "tensor"),
        P("expert", "tensor"),
        P("expert", "tensor"),
        P("tensor", "expert"),
        P("expert", None),
        P("expert", None),
        P("expert", "tensor", None),
        P("expert", None, "tensor"),
    )
    out_specs = (P("expert", "tensor"), P("expert", None, "tensor"), P("expert", None))
    return jax.shard_map(body, mesh=mesh, in_specs=in_specs, out_specs=out_specs, check_vma=False)
```

```python
import jax
import jax.numpy as jnp
import numpy as np
from jax import lax
from jax.experimental import pallas as pl
from jax.experimental.pallas import tpu as pltpu
from jax.sharding import PartitionSpec as P

MESH = pl.DeviceIdType.MESH
F32 = jnp.float32
BF16 = jnp.bfloat16
CAP = 5
BLK = 48
N_COPY = 160


def dot_nt(a, b):
    return lax.dot_general(a, b, (((1,), (1,)), ((), ())), preferred_element_type=F32)


def dot_tn(a, b):
    return lax.dot_general(a, b, (((0,), (0,)), ((), ())), preferred_element_type=F32)


def dot_nn(a, b):
    return jnp.dot(a, b, preferred_element_type=F32)


def tables():
    p2 = np.zeros((8 * BLK, 8 * BLK), np.float32)
    p3 = np.zeros((320, 8 * BLK), np.float32)
    p4 = np.zeros((64, 8 * BLK), np.float32)
    p5 = np.zeros((320, 128), np.float32)
    m5 = np.zeros((320, 128), np.float32)
    for h in range(2):
        for x in range(4):
            for z in range(8):
                j = h * 4 + x
                p2[x * 96 + 80 + h * 8 + z, z * BLK + 40 + j] = 1
                p4[h * 32 + z * 4 + x, x * 96 + 80 + h * 8 + z] = 1
                for s in range(CAP):
                    p2[x * 96 + h * 40 + z * CAP + s, z * BLK + j * CAP + s] = 1
                    p3[h * 160 + z * 20 + x * CAP + s, x * 96 + h * 40 + z * CAP + s] = 1
                    row = z * 40 + j * CAP + s
                    p5[row, h * 32 + z * 4 + x] = 1
                    m5[row, s] = 1
    return p2, p3, p4, p5, m5


def kernel(
    rw, grad_in, gate_in, up_in, wd_in, wg_in, wu_in, routes_in, ed_in, hid_in,
    p2_in, p3_in, p4_in, p5_in, m5_in,
    out_g, out_h, out_r,
    gate, up, routes, hid, p2, p3, p4, p5, m5,
    W, G, SL, S1, R1, S2, R2, DB, WR, WX, ED, half_acc, acc, K, XS, XR, YS, YR, RT0, RT1, ST2, RT2,
    ssem, rsem, lsem, xsend, xrecv, ysend, yrecv,
):
    e = lax.axis_index("expert")
    t = lax.axis_index("tensor")
    z = e // 8
    j = lax.rem(e, 8)
    yh = j // 4
    x = lax.rem(j, 4)
    yl = t // 2
    c = lax.rem(t, 2)
    yo = 1 - yh

    def zz(d):
        return lax.rem(z + d + 8, 8)

    def xx(d):
        return lax.rem(x + d, 4)

    def z_dev(d):
        return (zz(d) * 8 + j, t)

    def x_dev(d):
        return (z * 8 + yh * 4 + xx(d), t)

    def j_dev(d):
        return (z * 8 + lax.rem(j + d, 8), t)

    y_dev = (z * 8 + yo * 4 + x, t)
    sibling = (e, yl * 2 + 1 - c)

    def yl_dev(d):
        return (e, lax.rem(yl + d, 4) * 2 + c)

    def t_dev(d):
        return (e, lax.rem(t + d, 8))

    def far_dev(d):
        return (z * 8 + yo * 4 + x, lax.rem(yl + d, 4) * 2 + c)

    barrier = pltpu.get_barrier_semaphore()
    for d in range(1, 8):
        for dev in (z_dev(d), j_dev(d), t_dev(d)):
            pl.semaphore_signal(barrier, inc=1, device_id=dev, device_id_type=MESH)
    for d in range(1, 4):
        pl.semaphore_signal(barrier, inc=1, device_id=far_dev(d), device_id_type=MESH)

    local = {}

    def fetch(name, src, dst):
        copy = pltpu.make_async_copy(src, dst, lsem.at[len(local)])
        copy.start()
        local[name] = copy

    fetch("wd", wd_in, W.at[0, z, yh, x])
    fetch("wg", wg_in, W.at[1, z, yh, x])
    fetch("wu", wu_in, W.at[2, z, yh, x])
    fetch("grad", grad_in, G.at[t])
    fetch("routes", routes_in, routes)
    fetch("p2", p2_in, p2)
    fetch("p3", p3_in, p3)
    fetch("p4", p4_in, p4)
    fetch("p5", p5_in, p5)
    fetch("m5", m5_in, m5)
    fetch("gate", gate_in, gate)
    fetch("up", up_in, up)
    fetch("hid", hid_in, hid)
    fetch("ed", ed_in, ED)

    count = [0]
    sends = []

    def send(src, dst, dev):
        i = count[0]
        count[0] += 1
        copy = pltpu.make_async_remote_copy(
            src_ref=src, dst_ref=dst, send_sem=ssem.at[i], recv_sem=rsem.at[i],
            device_id=dev, device_id_type=MESH,
        )
        copy.start()
        sends.append(copy)
        return copy

    kinds = (pl.ds(0, 1), pl.ds(1, 2))

    def ring(kd, half, step, right):
        sign = 1 if right else -1
        zc = zz(-sign * (step - 1))
        if half == "own":
            ref = W.at[kinds[kd], zc, yh]
            if step == 4:
                ref = W.at[kinds[kd], zc, yh, pl.ds(0 if right else 2, 2)]
        else:
            ref = W.at[kinds[kd], zc, yo, x]
            if step == 4:
                ref = W.at[kinds[kd], zc, yo, x, pl.ds(0 if right else 32, 32)]
        return send(ref, ref, z_dev(sign))

    def x_send(kd, delta, half):
        ref = W.at[kinds[kd], zz(delta), half, x]
        return [send(ref, ref, x_dev(d)) for d in range(1, 4)]

    def gather_start(buf):
        own = buf.at[t]
        return [send(own, own, yl_dev(d)) for d in range(1, 4)] + [send(own, own, sibling)]

    def gather_forward(buf, first_copies):
        out = []
        for d in range(1, 4):
            first_copies[d - 1].wait_recv()
            ref = buf.at[lax.rem(yl - d + 4, 4) * 2 + c]
            out.append(send(ref, ref, sibling))
        return out

    a = {}
    b = {}
    ax = {}
    bx = {}

    def a_open(kd):
        across[kd].wait_recv()
        for right in (True, False):
            a[kd, 1, right] = ring(kd, "other", 1, right)
        ax[kd, 0] = x_send(kd, 0, yo)

    def a_step(kd, step):
        a[kd, step, True].wait_recv()
        if step < 4:
            a[kd, step + 1, True] = ring(kd, "other", step + 1, True)
        a[kd, step, False].wait_recv()
        if step < 4:
            a[kd, step + 1, False] = ring(kd, "other", step + 1, False)
            ax[kd, -step] = x_send(kd, -step, yo)
            ax[kd, step] = x_send(kd, step, yo)
        else:
            ax[kd, 4] = x_send(kd, 4, yo)

    def b_open(kd):
        for copy in bx[kd]:
            copy.wait_recv()
        for right in (True, False):
            b[kd, 1, right] = ring(kd, "own", 1, right)

    def b_step(kd, step):
        b[kd, step, True].wait_recv()
        if step < 4:
            b[kd, step + 1, True] = ring(kd, "own", step + 1, True)
        b[kd, step, False].wait_recv()
        if step < 4:
            b[kd, step + 1, False] = ring(kd, "own", step + 1, False)

    lane = lax.broadcasted_iota(jnp.int32, (128, 128), 1).astype(F32)
    row = lax.broadcasted_iota(jnp.int32, (128, 128), 0).astype(F32)
    lane_b = lax.broadcasted_iota(jnp.int32, (128, 8 * BLK), 1).astype(F32)
    local["routes"].wait()

    def column(values):
        return jnp.sum(jnp.where(lane == row, values, 0.0), axis=1, keepdims=True)

    high = [lax.shift_right_logical(routes[k : k + 1, :], 3) for k in range(2)]
    low = [lax.bitwise_and(routes[k : k + 1, :], 7) for k in range(2)]
    base = [column((high[k] * BLK + low[k] * CAP).astype(F32)) for k in range(2)]
    spare = [column((high[k] * BLK + low[k] + 40).astype(F32)) for k in range(2)]
    onehot = [(column(routes[k : k + 1, :].astype(F32)) == lane).astype(F32) for k in range(2)]
    lower = (lane < row).astype(BF16)
    earlier = dot_nn(lower, (onehot[0] + onehot[1]).astype(BF16))
    rank = [
        jnp.sum(earlier * onehot[0], axis=1, keepdims=True),
        jnp.sum((earlier + onehot[0]) * onehot[1], axis=1, keepdims=True),
    ]
    slot_map = jnp.zeros((128, 8 * BLK), F32)
    weight_rows = jnp.zeros((8 * BLK, 128), F32)
    for k in range(2):
        slot_map += (base[k] + rank[k] == lane_b).astype(F32)
        weight = column(rw[k : k + 1, :].astype(F32))
        value = jnp.where(lane == rank[k], weight, 0.0).astype(BF16)
        weight_rows += dot_tn((spare[k] == lane_b).astype(BF16), value)
    local["grad"].wait()
    filled = dot_tn(slot_map.astype(BF16), G[t])
    first = (filled[:, 0:128] + weight_rows).astype(BF16)
    for k in range(8):
        S1[k, :, 0:128] = first[k * BLK : (k + 1) * BLK]
        S1[k, :, 128:512] = filled[k * BLK : (k + 1) * BLK, 128:512].astype(BF16)
    R1[z] = S1[z]

    pl.semaphore_wait(barrier, 24)
    disp1 = [send(S1.at[zz(d)], R1.at[z], z_dev(d)) for d in range(1, 8)]
    local["wd"].wait()
    local["wg"].wait()
    local["wu"].wait()
    across = {}
    for kd in range(2):
        ref = W.at[kinds[kd], z, yh, x]
        bx[kd] = x_send(kd, 0, yh)
        across[kd] = send(ref, ref, y_dev)
    tok = gather_start(G)
    local["p2"].wait()
    for copy in disp1:
        copy.wait_recv()
    shuffled = dot_nn(p2[...], R1[...].reshape(8 * BLK, 512)).astype(BF16)
    S2[...] = shuffled.reshape(4, 96, 512)
    R2[x] = S2[x]
    disp2 = [send(S2.at[xx(d)], R2.at[x], x_dev(d)) for d in range(1, 4)]
    b_open(0)
    b_open(1)

    a_open(0)
    b_step(0, 1)
    a_open(1)
    a_step(0, 1)
    tok_fwd = gather_forward(G, tok)

    a_step(1, 1)
    for name in ("p3", "p4", "p5", "m5"):
        local[name].wait()
    for copy in disp2:
        copy.wait_recv()
    arrived = R2[...].reshape(8 * BLK, 512)
    DB[...] = dot_nn(p3[...], arrived).astype(BF16).reshape(2, 160, 512)
    WR[...] = dot_nn(p4[...], arrived[:, 0:128]).astype(BF16).reshape(2, 32, 128)
    SL[yh, t] = DB[yh]
    mine = SL.at[yh, t]
    near = [send(mine, mine, yl_dev(d)) for d in range(1, 4)]
    far = [send(DB.at[yo], mine, far_dev(d)) for d in range(4)]
    twin = [send(mine, mine, sibling)]
    weights_far = send(WR.at[yo], WX, y_dev)
    sends.pop()

    b_step(0, 2)
    a_step(0, 2)
    b_step(1, 1)
    a_step(1, 2)
    b_step(0, 3)
    a_step(0, 3)
    a_step(1, 3)
    a_step(0, 4)
    b_step(0, 4)
    a_step(1, 4)
    b_step(1, 2)

    for name in ("hid", "ed"):
        local[name].wait()
    def expert_term(h, idx):
        cols = pl.ds(pl.multiple_of(idx * 512, 512), 512)
        return dot_nt(SL[h, idx], ED[:, cols])

    half_acc[yh] = expert_term(yh, t)
    for d in range(1, 4):
        near[d - 1].wait_recv()
        idx = lax.rem(yl - d + 4, 4) * 2 + c
        twin.append(send(SL.at[yh, idx], SL.at[yh, idx], sibling))
        half_acc[yh] += expert_term(yh, idx)
    for d in range(4):
        far[d].wait_recv()
        idx = lax.rem(yl - d + 4, 4) * 2 + c
        twin.append(send(SL.at[yo, idx], SL.at[yo, idx], sibling))
        if d == 0:
            half_acc[yo] = expert_term(yo, idx)
        else:
            half_acc[yo] += expert_term(yo, idx)
    for d in range(4):
        twin[d].wait_recv()
        half_acc[yh] += expert_term(yh, lax.rem(yl - d + 4, 4) * 2 + 1 - c)
    for d in range(4):
        twin[4 + d].wait_recv()
        half_acc[yo] += expert_term(yo, lax.rem(yl - d + 4, 4) * 2 + 1 - c)
    for h in range(2):
        for k in range(8):
            acc[k * 40 + h * 20 : k * 40 + h * 20 + 20, :] = half_acc[h, k * 20 : k * 20 + 20, :]
    weights_far.wait()
    WR[yo] = WX[...]
    all_weights = jnp.concatenate(
        [WR[...].reshape(64, 128), jnp.zeros((64, 128), BF16)], axis=0
    )
    slot_weight = jnp.sum(dot_nn(p5[...], all_weights) * m5[...], axis=1, keepdims=True)
    out_h[...] = (slot_weight * acc[...]).astype(BF16)
    products = jnp.sum(hid[...].astype(F32) * acc[...], axis=1, keepdims=True)
    diag = lax.broadcasted_iota(jnp.int32, (40, 128), 0) == lax.broadcasted_iota(
        jnp.int32, (40, 128), 1
    )
    tile = jnp.concatenate(
        [
            jnp.sum(jnp.where(diag, products[k * 40 : (k + 1) * 40], 0.0), axis=0, keepdims=True)
            for k in range(8)
        ],
        axis=0,
    )
    RT0[t] = tile
    own = RT0.at[t]
    ret0 = [send(own, own, t_dev(d)) for d in range(1, 8)]

    tok[3].wait_recv()
    for copy in tok_fwd:
        copy.wait_recv()
    for delta in (0, -1, 1, -2, 2, -3, 3, 4):
        for copy in ax[0, delta]:
            copy.wait_recv()
    for name in ("gate", "up"):
        local[name].wait()
    hd = jnp.zeros((128, 384), F32)
    for k in range(8):
        hd += dot_nn(G[k], W[0, k].reshape(512, 384))
    gate_f = gate[...].astype(F32)
    up_f = up[...].astype(F32)
    sig = jax.nn.sigmoid(gate_f)
    swish = gate_f * sig
    slope = sig * (1.0 + gate_f * (1.0 - sig))
    gd = (hd * up_f * slope).astype(BF16)
    ud = (hd * swish).astype(BF16)

    def sib_copy(zb):
        return pltpu.make_async_remote_copy(
            src_ref=XS.at[zb], dst_ref=XR.at[zb], send_sem=xsend.at[zb], recv_sem=xrecv.at[zb],
            device_id=sibling, device_id_type=MESH,
        )

    def y_copy(zb, src):
        return pltpu.make_async_remote_copy(
            src_ref=YS.at[zb], dst_ref=YR.at[src], send_sem=ysend.at[zb], recv_sem=yrecv.at[src],
            device_id=(e, zb), device_id_type=MESH,
        )

    def part(delta):
        zb = zz(delta)
        for copy in ax[1, delta]:
            copy.wait_recv()
        value = dot_nt(gd, W[1, zb].reshape(512, 384)) + dot_nt(ud, W[2, zb].reshape(512, 384))

        @pl.when(lax.rem(zb, 2) == c)
        def _():
            K[zb] = value

        @pl.when(lax.rem(zb, 2) != c)
        def _():
            XS[zb] = value.astype(BF16)
            sib_copy(zb).start()

    def pass_on(delta):
        zb = zz(delta)

        @pl.when(lax.rem(zb, 2) == c)
        def _():
            sib_copy(zb).wait_recv()
            K[zb] = K[zb] + XR[zb].astype(F32)

            @pl.when(zb != t)
            def _():
                YS[zb] = K[zb].astype(BF16)
                y_copy(zb, yl).start()

    for copy in ret0:
        copy.wait_recv()
    RT1[j] = jnp.sum(RT0[...], axis=0)
    own1 = RT1.at[j]
    ret1 = [send(own1, own1, j_dev(d)) for d in range(1, 8)]
    part(0)
    part(-1)
    pass_on(0)
    part(1)
    pass_on(-1)
    pass_on(1)
    for copy in ret1:
        copy.wait_recv()
    for k in range(8):
        ST2[k] = RT1[:, k, :]
    RT2[z] = ST2[z]
    ret2 = [send(ST2.at[zz(d)], RT2.at[z], z_dev(d)) for d in range(1, 8)]
    part(-2)
    part(2)
    pass_on(-2)
    b_step(1, 3)
    pass_on(2)
    for copy in ret2:
        copy.wait_recv()
    back = RT2[...].reshape(64, 128)
    jf = (j * CAP).astype(F32)
    for k in range(2):
        scores = jnp.dot(
            onehot[k][:, 0:64], back, preferred_element_type=F32, precision=lax.Precision.HIGHEST
        )
        score = jnp.sum(jnp.where(lane == rank[k] + jf, scores, 0.0), axis=1, keepdims=True)
        out_r[k : k + 1, :] = jnp.sum(jnp.where(lane == row, score, 0.0), axis=0, keepdims=True)

    part(-3)
    part(3)
    pass_on(-3)
    b_step(1, 4)
    pass_on(3)
    part(4)
    pass_on(4)
    total = K[t]
    for d in range(1, 4):
        src = lax.rem(yl + d, 4)
        y_copy(t, src).wait_recv()
        total += YR[src].astype(F32)
    out_g[...] = total.astype(BF16)
    for d in range(1, 4):
        y_copy(lax.rem(yl + d, 4) * 2 + c, yl).wait_send()
    for q in range(4):
        sib_copy(q * 2 + 1 - c).wait_send()
    for copy in sends:
        copy.wait_send()


def body(
    grad_out, dense_gate, dense_up, w_gate, w_up, w_down, routes, route_weight,
    expert_down, expert_hidden,
):
    p2, p3, p4, p5, m5 = tables()
    vmem = pl.BlockSpec(memory_space=pltpu.VMEM)
    hbm = pl.BlockSpec(memory_space=pltpu.HBM)
    out_g, out_h, out_r = pl.pallas_call(
        kernel,
        out_shape=(
            jax.ShapeDtypeStruct((128, 512), BF16),
            jax.ShapeDtypeStruct((320, 384), BF16),
            jax.ShapeDtypeStruct((2, 128), F32),
        ),
        in_specs=[vmem] + [hbm] * 14,
        out_specs=(vmem, vmem, vmem),
        scratch_shapes=[
            pltpu.VMEM((128, 384), BF16),
            pltpu.VMEM((128, 384), BF16),
            pltpu.VMEM((2, 128), jnp.int32),
            pltpu.VMEM((320, 384), BF16),
            pltpu.VMEM((8 * BLK, 8 * BLK), BF16),
            pltpu.VMEM((320, 8 * BLK), BF16),
            pltpu.VMEM((64, 8 * BLK), BF16),
            pltpu.VMEM((320, 128), BF16),
            pltpu.VMEM((320, 128), F32),
            pltpu.VMEM((3, 8, 2, 4, 64, 384), BF16),
            pltpu.VMEM((8, 128, 512), BF16),
            pltpu.VMEM((2, 8, 160, 512), BF16),
            pltpu.VMEM((8, BLK, 512), BF16),
            pltpu.VMEM((8, BLK, 512), BF16),
            pltpu.VMEM((4, 96, 512), BF16),
            pltpu.VMEM((4, 96, 512), BF16),
            pltpu.VMEM((2, 160, 512), BF16),
            pltpu.VMEM((2, 32, 128), BF16),
            pltpu.VMEM((32, 128), BF16),
            pltpu.VMEM((384, 4096), BF16),
            pltpu.VMEM((2, 160, 384), F32),
            pltpu.VMEM((320, 384), F32),
            pltpu.VMEM((8, 128, 512), F32),
            pltpu.VMEM((8, 128, 512), BF16),
            pltpu.VMEM((8, 128, 512), BF16),
            pltpu.VMEM((8, 128, 512), BF16),
            pltpu.VMEM((4, 128, 512), BF16),
            pltpu.VMEM((8, 8, 128), F32),
            pltpu.VMEM((8, 8, 128), F32),
            pltpu.VMEM((8, 8, 128), F32),
            pltpu.VMEM((8, 8, 128), F32),
            pltpu.SemaphoreType.DMA((N_COPY,)),
            pltpu.SemaphoreType.DMA((N_COPY,)),
            pltpu.SemaphoreType.DMA((16,)),
            pltpu.SemaphoreType.DMA((8,)),
            pltpu.SemaphoreType.DMA((8,)),
            pltpu.SemaphoreType.DMA((8,)),
            pltpu.SemaphoreType.DMA((4,)),
        ],
        compiler_params=pltpu.CompilerParams(
            collective_id=0, has_side_effects=True, vmem_limit_bytes=60 << 20
        ),
    )(
        route_weight.T, grad_out, dense_gate, dense_up, w_down.T, w_gate, w_up, routes.T,
        expert_down[0], expert_hidden[0],
        jnp.asarray(p2, BF16), jnp.asarray(p3, BF16), jnp.asarray(p4, BF16), jnp.asarray(p5, BF16),
        jnp.asarray(m5, F32),
    )
    return out_g, out_h[None], out_r.T


def solution(mesh):
    in_specs = (
        P("expert", "tensor"),
        P("expert", "tensor"),
        P("expert", "tensor"),
        P("expert", "tensor"),
        P("expert", "tensor"),
        P("tensor", "expert"),
        P("expert", None),
        P("expert", None),
        P("expert", "tensor", None),
        P("expert", None, "tensor"),
    )
    out_specs = (P("expert", "tensor"), P("expert", None, "tensor"), P("expert", None))
    return jax.shard_map(body, mesh=mesh, in_specs=in_specs, out_specs=out_specs, check_vma=False)
```

```python
import jax
import jax.numpy as jnp
import numpy as np
from jax import lax
from jax.experimental import pallas as pl
from jax.experimental.pallas import tpu as pltpu
from jax.sharding import PartitionSpec as P

MESH = pl.DeviceIdType.MESH
F32 = jnp.float32
BF16 = jnp.bfloat16
CAP = 5
BLK = 48
N_COPY = 224


def dot_nt(a, b):
    return lax.dot_general(a, b, (((1,), (1,)), ((), ())), preferred_element_type=F32)


def dot_tn(a, b):
    return lax.dot_general(a, b, (((0,), (0,)), ((), ())), preferred_element_type=F32)


def dot_nn(a, b):
    return jnp.dot(a, b, preferred_element_type=F32)


def tables():
    p2 = np.zeros((8 * BLK, 8 * BLK), np.float32)
    p3 = np.zeros((320, 8 * BLK), np.float32)
    p4 = np.zeros((64, 8 * BLK), np.float32)
    p5 = np.zeros((320, 128), np.float32)
    m5 = np.zeros((320, 128), np.float32)
    for h in range(2):
        for x in range(4):
            for z in range(8):
                j = h * 4 + x
                p2[x * 96 + 80 + h * 8 + z, z * BLK + 40 + j] = 1
                p4[h * 32 + z * 4 + x, x * 96 + 80 + h * 8 + z] = 1
                for s in range(CAP):
                    p2[x * 96 + h * 40 + z * CAP + s, z * BLK + j * CAP + s] = 1
                    p3[h * 160 + z * 20 + x * CAP + s, x * 96 + h * 40 + z * CAP + s] = 1
                    row = z * 40 + j * CAP + s
                    p5[row, h * 32 + z * 4 + x] = 1
                    m5[row, s] = 1
    return p2, p3, p4, p5, m5


def kernel(
    rw, grad_in, gate_in, up_in, wd_in, wg_in, wu_in, routes_in, ed_in, hid_in,
    p2_in, p3_in, p4_in, p5_in, m5_in,
    out_g, out_h, out_r,
    gate, up, routes, hid, p2, p3, p4, p5, m5,
    W, G, SL, S1, R1, S2, R2, DB, WR, WX, ED, half_acc, acc, K, XS, XR, YS, YR, RT0, RT1, ST2, RT2,
    ssem, rsem, lsem, xsend, xrecv, ysend, yrecv,
):
    e = lax.axis_index("expert")
    t = lax.axis_index("tensor")
    z = e // 8
    j = lax.rem(e, 8)
    yh = j // 4
    x = lax.rem(j, 4)
    yl = t // 2
    c = lax.rem(t, 2)
    yo = 1 - yh

    def zz(d):
        return lax.rem(z + d + 8, 8)

    def xx(d):
        return lax.rem(x + d, 4)

    def z_dev(d):
        return (zz(d) * 8 + j, t)

    def x_dev(d):
        return (z * 8 + yh * 4 + xx(d), t)

    def j_dev(d):
        return (z * 8 + lax.rem(j + d, 8), t)

    y_dev = (z * 8 + yo * 4 + x, t)
    sibling = (e, yl * 2 + 1 - c)

    def yl_dev(d):
        return (e, lax.rem(yl + d, 4) * 2 + c)

    def t_dev(d):
        return (e, lax.rem(t + d, 8))

    def far_dev(d):
        return (z * 8 + yo * 4 + x, lax.rem(yl + d, 4) * 2 + c)

    barrier = pltpu.get_barrier_semaphore()
    for d in range(1, 8):
        for dev in (z_dev(d), j_dev(d), t_dev(d)):
            pl.semaphore_signal(barrier, inc=1, device_id=dev, device_id_type=MESH)
    for d in range(1, 4):
        pl.semaphore_signal(barrier, inc=1, device_id=far_dev(d), device_id_type=MESH)

    local = {}

    def fetch(name, src, dst):
        copy = pltpu.make_async_copy(src, dst, lsem.at[len(local)])
        copy.start()
        local[name] = copy

    fetch("wd", wd_in, W.at[0, z, yh, x])
    fetch("wg", wg_in, W.at[1, z, yh, x])
    fetch("wu", wu_in, W.at[2, z, yh, x])
    fetch("grad", grad_in, G.at[t])
    fetch("routes", routes_in, routes)
    fetch("p2", p2_in, p2)
    fetch("p3", p3_in, p3)
    fetch("p4", p4_in, p4)
    fetch("p5", p5_in, p5)
    fetch("m5", m5_in, m5)
    fetch("gate", gate_in, gate)
    fetch("up", up_in, up)
    fetch("hid", hid_in, hid)
    fetch("ed", ed_in, ED)

    count = [0]
    sends = []

    def send(src, dst, dev):
        i = count[0]
        count[0] += 1
        copy = pltpu.make_async_remote_copy(
            src_ref=src, dst_ref=dst, send_sem=ssem.at[i], recv_sem=rsem.at[i],
            device_id=dev, device_id_type=MESH,
        )
        copy.start()
        sends.append(copy)
        return copy

    kinds = (pl.ds(0, 1), pl.ds(1, 2))

    def ring(key, step, right):
        sign = 1 if right else -1
        zc = zz(-sign * (step - 1))
        if key == "own":
            ref = W.at[kinds[1], zc, yh]
            if step == 4:
                ref = W.at[kinds[1], zc, yh, pl.ds(0 if right else 2, 2)]
        else:
            kd, far_half = key
            half = yo if far_half else yh
            ref = W.at[kinds[kd], zc, half, x]
            if step == 4:
                ref = W.at[kinds[kd], zc, half, x, pl.ds(0 if right else 32, 32)]
        return send(ref, ref, z_dev(sign))

    def x_send(key, delta):
        kd, far_half = key
        ref = W.at[kinds[kd], zz(delta), yo if far_half else yh, x]
        return [send(ref, ref, x_dev(1)), send(ref, ref, x_dev(3))]

    def x_relay(key, delta):
        kd, far_half = key
        block = W.at[kinds[kd], zz(delta), yo if far_half else yh]
        ax[key, delta][0].wait_recv()
        low = block.at[:, xx(3), pl.ds(0, 32)]
        relay = [send(low, low, x_dev(1))]
        ax[key, delta][1].wait_recv()
        high = block.at[:, xx(1), pl.ds(32, 32)]
        relay.append(send(high, high, x_dev(3)))
        ar[key, delta] = relay

    def gather_start(buf):
        own = buf.at[t]
        return [send(own, own, yl_dev(d)) for d in range(1, 4)] + [send(own, own, sibling)]

    def gather_forward(buf, first_copies):
        out = []
        for d in range(1, 4):
            first_copies[d - 1].wait_recv()
            ref = buf.at[lax.rem(yl - d + 4, 4) * 2 + c]
            out.append(send(ref, ref, sibling))
        return out

    a = {}
    b = {}
    ax = {}
    ar = {}
    down_own, down_far, wide_far = (0, False), (0, True), (1, True)

    def a_open(key):
        if key[1]:
            across[key[0]].wait_recv()
        for right in (True, False):
            a[key, 1, right] = ring(key, 1, right)
        ax[key, 0] = x_send(key, 0)

    def a_step(key, step):
        a[key, step, True].wait_recv()
        if step < 4:
            a[key, step + 1, True] = ring(key, step + 1, True)
        a[key, step, False].wait_recv()
        if step < 4:
            a[key, step + 1, False] = ring(key, step + 1, False)
            ax[key, -step] = x_send(key, -step)
            ax[key, step] = x_send(key, step)
        else:
            ax[key, 4] = x_send(key, 4)

    def relay_step(key, step):
        if step in (0, 4):
            x_relay(key, step)
        else:
            x_relay(key, -step)
            x_relay(key, step)

    def b_open():
        for copy in bx:
            copy.wait_recv()
        for right in (True, False):
            b[1, right] = ring("own", 1, right)

    def b_step(step):
        b[step, True].wait_recv()
        if step < 4:
            b[step + 1, True] = ring("own", step + 1, True)
        b[step, False].wait_recv()
        if step < 4:
            b[step + 1, False] = ring("own", step + 1, False)

    lane = lax.broadcasted_iota(jnp.int32, (128, 128), 1).astype(F32)
    row = lax.broadcasted_iota(jnp.int32, (128, 128), 0).astype(F32)
    lane_b = lax.broadcasted_iota(jnp.int32, (128, 8 * BLK), 1).astype(F32)
    local["routes"].wait()

    def column(values):
        return jnp.sum(jnp.where(lane == row, values, 0.0), axis=1, keepdims=True)

    high = [lax.shift_right_logical(routes[k : k + 1, :], 3) for k in range(2)]
    low = [lax.bitwise_and(routes[k : k + 1, :], 7) for k in range(2)]
    base = [column((high[k] * BLK + low[k] * CAP).astype(F32)) for k in range(2)]
    spare = [column((high[k] * BLK + low[k] + 40).astype(F32)) for k in range(2)]
    onehot = [(column(routes[k : k + 1, :].astype(F32)) == lane).astype(F32) for k in range(2)]
    lower = (lane < row).astype(BF16)
    earlier = dot_nn(lower, (onehot[0] + onehot[1]).astype(BF16))
    rank = [
        jnp.sum(earlier * onehot[0], axis=1, keepdims=True),
        jnp.sum((earlier + onehot[0]) * onehot[1], axis=1, keepdims=True),
    ]
    slot_map = jnp.zeros((128, 8 * BLK), F32)
    weight_rows = jnp.zeros((8 * BLK, 128), F32)
    for k in range(2):
        slot_map += (base[k] + rank[k] == lane_b).astype(F32)
        weight = column(rw[k : k + 1, :].astype(F32))
        value = jnp.where(lane == rank[k], weight, 0.0).astype(BF16)
        weight_rows += dot_tn((spare[k] == lane_b).astype(BF16), value)
    local["grad"].wait()
    filled = dot_tn(slot_map.astype(BF16), G[t])
    first = (filled[:, 0:128] + weight_rows).astype(BF16)
    for k in range(8):
        S1[k, :, 0:128] = first[k * BLK : (k + 1) * BLK]
        S1[k, :, 128:512] = filled[k * BLK : (k + 1) * BLK, 128:512].astype(BF16)
    R1[z] = S1[z]

    pl.semaphore_wait(barrier, 24)
    local["wd"].wait()
    local["wg"].wait()
    local["wu"].wait()
    a_open(down_own)
    ref = W.at[kinds[1], z, yh, x]
    bx = [send(ref, ref, x_dev(d)) for d in range(1, 4)]
    across = []
    for kd in range(2):
        ref = W.at[kinds[kd], z, yh, x]
        across.append(send(ref, ref, y_dev))
    disp1 = [send(S1.at[zz(d)], R1.at[z], z_dev(d)) for d in range(1, 8)]
    tok = gather_start(G)
    local["p2"].wait()
    for copy in disp1:
        copy.wait_recv()
    shuffled = dot_nn(p2[...], R1[...].reshape(8 * BLK, 512)).astype(BF16)
    S2[...] = shuffled.reshape(4, 96, 512)
    R2[x] = S2[x]
    disp2 = [send(S2.at[xx(d)], R2.at[x], x_dev(d)) for d in range(1, 4)]
    a_step(down_own, 1)
    b_open()
    a_open(down_far)
    a_open(wide_far)
    a_step(down_own, 2)
    tok_fwd = gather_forward(G, tok)

    for name in ("p3", "p4", "p5", "m5"):
        local[name].wait()
    for copy in disp2:
        copy.wait_recv()
    arrived = R2[...].reshape(8 * BLK, 512)
    DB[...] = dot_nn(p3[...], arrived).astype(BF16).reshape(2, 160, 512)
    WR[...] = dot_nn(p4[...], arrived[:, 0:128]).astype(BF16).reshape(2, 32, 128)
    SL[yh, t] = DB[yh]
    mine = SL.at[yh, t]
    near = [send(mine, mine, yl_dev(d)) for d in range(1, 4)]
    far = [send(DB.at[yo], mine, far_dev(d)) for d in range(4)]
    twin = [send(mine, mine, sibling)]
    weights_far = send(WR.at[yo], WX, y_dev)
    sends.pop()

    a_step(down_far, 1)
    a_step(wide_far, 1)
    a_step(down_own, 3)
    a_step(down_far, 2)
    a_step(down_own, 4)
    relay_step(down_own, 0)
    b_step(1)
    a_step(wide_far, 2)
    relay_step(down_own, 1)
    relay_step(down_far, 0)
    a_step(down_far, 3)
    relay_step(wide_far, 0)
    relay_step(down_own, 2)
    relay_step(down_far, 1)
    a_step(wide_far, 3)
    a_step(down_far, 4)
    b_step(2)
    relay_step(down_own, 3)
    relay_step(wide_far, 1)
    relay_step(down_far, 2)
    a_step(wide_far, 4)
    relay_step(down_own, 4)
    relay_step(down_far, 3)
    relay_step(wide_far, 2)
    relay_step(down_far, 4)
    relay_step(wide_far, 3)

    for name in ("hid", "ed"):
        local[name].wait()
    def expert_term(h, idx):
        cols = pl.ds(pl.multiple_of(idx * 512, 512), 512)
        return dot_nt(SL[h, idx], ED[:, cols])

    half_acc[yh] = expert_term(yh, t)
    for d in range(1, 4):
        near[d - 1].wait_recv()
        idx = lax.rem(yl - d + 4, 4) * 2 + c
        twin.append(send(SL.at[yh, idx], SL.at[yh, idx], sibling))
        half_acc[yh] += expert_term(yh, idx)
    for d in range(4):
        far[d].wait_recv()
        idx = lax.rem(yl - d + 4, 4) * 2 + c
        twin.append(send(SL.at[yo, idx], SL.at[yo, idx], sibling))
        if d == 0:
            half_acc[yo] = expert_term(yo, idx)
        else:
            half_acc[yo] += expert_term(yo, idx)
    for d in range(4):
        twin[d].wait_recv()
        half_acc[yh] += expert_term(yh, lax.rem(yl - d + 4, 4) * 2 + 1 - c)
    for d in range(4):
        twin[4 + d].wait_recv()
        half_acc[yo] += expert_term(yo, lax.rem(yl - d + 4, 4) * 2 + 1 - c)
    for h in range(2):
        for k in range(8):
            acc[k * 40 + h * 20 : k * 40 + h * 20 + 20, :] = half_acc[h, k * 20 : k * 20 + 20, :]
    weights_far.wait()
    WR[yo] = WX[...]
    all_weights = jnp.concatenate(
        [WR[...].reshape(64, 128), jnp.zeros((64, 128), BF16)], axis=0
    )
    slot_weight = jnp.sum(dot_nn(p5[...], all_weights) * m5[...], axis=1, keepdims=True)
    out_h[...] = (slot_weight * acc[...]).astype(BF16)
    products = jnp.sum(hid[...].astype(F32) * acc[...], axis=1, keepdims=True)
    diag = lax.broadcasted_iota(jnp.int32, (40, 128), 0) == lax.broadcasted_iota(
        jnp.int32, (40, 128), 1
    )
    tile = jnp.concatenate(
        [
            jnp.sum(jnp.where(diag, products[k * 40 : (k + 1) * 40], 0.0), axis=0, keepdims=True)
            for k in range(8)
        ],
        axis=0,
    )
    RT0[t] = tile
    own = RT0.at[t]
    ret0 = [send(own, own, t_dev(d)) for d in range(1, 8)]

    b_step(3)

    tok[3].wait_recv()
    for copy in tok_fwd:
        copy.wait_recv()
    for delta in (0, -1, 1, -2, 2, -3, 3, 4):
        for copy in ar[down_own, delta] + ar[down_far, delta]:
            copy.wait_recv()
    for name in ("gate", "up"):
        local[name].wait()
    hd = jnp.zeros((128, 384), F32)
    for k in range(8):
        hd += dot_nn(G[k], W[0, k].reshape(512, 384))
    gate_f = gate[...].astype(F32)
    up_f = up[...].astype(F32)
    sig = jax.nn.sigmoid(gate_f)
    swish = gate_f * sig
    slope = sig * (1.0 + gate_f * (1.0 - sig))
    gd = (hd * up_f * slope).astype(BF16)
    ud = (hd * swish).astype(BF16)

    def sib_copy(zb):
        return pltpu.make_async_remote_copy(
            src_ref=XS.at[zb], dst_ref=XR.at[zb], send_sem=xsend.at[zb], recv_sem=xrecv.at[zb],
            device_id=sibling, device_id_type=MESH,
        )

    def y_copy(zb, src):
        return pltpu.make_async_remote_copy(
            src_ref=YS.at[zb], dst_ref=YR.at[src], send_sem=ysend.at[zb], recv_sem=yrecv.at[src],
            device_id=(e, zb), device_id_type=MESH,
        )

    def part(delta):
        zb = zz(delta)
        for copy in ar[wide_far, delta]:
            copy.wait_recv()
        value = dot_nt(gd, W[1, zb].reshape(512, 384)) + dot_nt(ud, W[2, zb].reshape(512, 384))

        @pl.when(lax.rem(zb, 2) == c)
        def _():
            K[zb] = value

        @pl.when(lax.rem(zb, 2) != c)
        def _():
            XS[zb] = value.astype(BF16)
            sib_copy(zb).start()

    def pass_on(delta):
        zb = zz(delta)

        @pl.when(lax.rem(zb, 2) == c)
        def _():
            sib_copy(zb).wait_recv()
            K[zb] = K[zb] + XR[zb].astype(F32)

            @pl.when(zb != t)
            def _():
                YS[zb] = K[zb].astype(BF16)
                y_copy(zb, yl).start()

    for copy in ret0:
        copy.wait_recv()
    RT1[j] = jnp.sum(RT0[...], axis=0)
    own1 = RT1.at[j]
    ret1 = [send(own1, own1, j_dev(d)) for d in range(1, 8)]
    part(0)
    part(-1)
    pass_on(0)
    part(1)
    pass_on(-1)
    pass_on(1)
    for copy in ret1:
        copy.wait_recv()
    for k in range(8):
        ST2[k] = RT1[:, k, :]
    RT2[z] = ST2[z]
    ret2 = [send(ST2.at[zz(d)], RT2.at[z], z_dev(d)) for d in range(1, 8)]
    part(-2)
    part(2)
    pass_on(-2)
    pass_on(2)
    for copy in ret2:
        copy.wait_recv()
    back = RT2[...].reshape(64, 128)
    jf = (j * CAP).astype(F32)
    for k in range(2):
        scores = jnp.dot(
            onehot[k][:, 0:64], back, preferred_element_type=F32, precision=lax.Precision.HIGHEST
        )
        score = jnp.sum(jnp.where(lane == rank[k] + jf, scores, 0.0), axis=1, keepdims=True)
        out_r[k : k + 1, :] = jnp.sum(jnp.where(lane == row, score, 0.0), axis=0, keepdims=True)

    part(-3)
    part(3)
    pass_on(-3)
    x_relay(wide_far, 4)
    b_step(4)
    pass_on(3)
    part(4)
    pass_on(4)
    total = K[t]
    for d in range(1, 4):
        src = lax.rem(yl + d, 4)
        y_copy(t, src).wait_recv()
        total += YR[src].astype(F32)
    out_g[...] = total.astype(BF16)
    for d in range(1, 4):
        y_copy(lax.rem(yl + d, 4) * 2 + c, yl).wait_send()
    for q in range(4):
        sib_copy(q * 2 + 1 - c).wait_send()
    for copy in sends:
        copy.wait_send()


def body(
    grad_out, dense_gate, dense_up, w_gate, w_up, w_down, routes, route_weight,
    expert_down, expert_hidden,
):
    p2, p3, p4, p5, m5 = tables()
    vmem = pl.BlockSpec(memory_space=pltpu.VMEM)
    hbm = pl.BlockSpec(memory_space=pltpu.HBM)
    out_g, out_h, out_r = pl.pallas_call(
        kernel,
        out_shape=(
            jax.ShapeDtypeStruct((128, 512), BF16),
            jax.ShapeDtypeStruct((320, 384), BF16),
            jax.ShapeDtypeStruct((2, 128), F32),
        ),
        in_specs=[vmem] + [hbm] * 14,
        out_specs=(vmem, vmem, vmem),
        scratch_shapes=[
            pltpu.VMEM((128, 384), BF16),
            pltpu.VMEM((128, 384), BF16),
            pltpu.VMEM((2, 128), jnp.int32),
            pltpu.VMEM((320, 384), BF16),
            pltpu.VMEM((8 * BLK, 8 * BLK), BF16),
            pltpu.VMEM((320, 8 * BLK), BF16),
            pltpu.VMEM((64, 8 * BLK), BF16),
            pltpu.VMEM((320, 128), BF16),
            pltpu.VMEM((320, 128), F32),
            pltpu.VMEM((3, 8, 2, 4, 64, 384), BF16),
            pltpu.VMEM((8, 128, 512), BF16),
            pltpu.VMEM((2, 8, 160, 512), BF16),
            pltpu.VMEM((8, BLK, 512), BF16),
            pltpu.VMEM((8, BLK, 512), BF16),
            pltpu.VMEM((4, 96, 512), BF16),
            pltpu.VMEM((4, 96, 512), BF16),
            pltpu.VMEM((2, 160, 512), BF16),
            pltpu.VMEM((2, 32, 128), BF16),
            pltpu.VMEM((32, 128), BF16),
            pltpu.VMEM((384, 4096), BF16),
            pltpu.VMEM((2, 160, 384), F32),
            pltpu.VMEM((320, 384), F32),
            pltpu.VMEM((8, 128, 512), F32),
            pltpu.VMEM((8, 128, 512), BF16),
            pltpu.VMEM((8, 128, 512), BF16),
            pltpu.VMEM((8, 128, 512), BF16),
            pltpu.VMEM((4, 128, 512), BF16),
            pltpu.VMEM((8, 8, 128), F32),
            pltpu.VMEM((8, 8, 128), F32),
            pltpu.VMEM((8, 8, 128), F32),
            pltpu.VMEM((8, 8, 128), F32),
            pltpu.SemaphoreType.DMA((N_COPY,)),
            pltpu.SemaphoreType.DMA((N_COPY,)),
            pltpu.SemaphoreType.DMA((16,)),
            pltpu.SemaphoreType.DMA((8,)),
            pltpu.SemaphoreType.DMA((8,)),
            pltpu.SemaphoreType.DMA((8,)),
            pltpu.SemaphoreType.DMA((4,)),
        ],
        compiler_params=pltpu.CompilerParams(
            collective_id=0, has_side_effects=True, vmem_limit_bytes=60 << 20
        ),
    )(
        route_weight.T, grad_out, dense_gate, dense_up, w_down.T, w_gate, w_up, routes.T,
        expert_down[0], expert_hidden[0],
        jnp.asarray(p2, BF16), jnp.asarray(p3, BF16), jnp.asarray(p4, BF16), jnp.asarray(p5, BF16),
        jnp.asarray(m5, F32),
    )
    return out_g, out_h[None], out_r.T


def solution(mesh):
    in_specs = (
        P("expert", "tensor"),
        P("expert", "tensor"),
        P("expert", "tensor"),
        P("expert", "tensor"),
        P("expert", "tensor"),
        P("tensor", "expert"),
        P("expert", None),
        P("expert", None),
        P("expert", "tensor", None),
        P("expert", None, "tensor"),
    )
    out_specs = (P("expert", "tensor"), P("expert", None, "tensor"), P("expert", None))
    return jax.shard_map(body, mesh=mesh, in_specs=in_specs, out_specs=out_specs, check_vma=False)
```

```python
import jax
import jax.numpy as jnp
import numpy as np
from jax import lax
from jax.experimental import pallas as pl
from jax.experimental.pallas import tpu as pltpu
from jax.sharding import PartitionSpec as P

MESH = pl.DeviceIdType.MESH
F32 = jnp.float32
BF16 = jnp.bfloat16
CAP = 5
BLK = 48
N_COPY = 224


def dot_nt(a, b):
    return lax.dot_general(a, b, (((1,), (1,)), ((), ())), preferred_element_type=F32)


def dot_tn(a, b):
    return lax.dot_general(a, b, (((0,), (0,)), ((), ())), preferred_element_type=F32)


def dot_nn(a, b):
    return jnp.dot(a, b, preferred_element_type=F32)


def tables():
    p2 = np.zeros((8 * BLK, 8 * BLK), np.float32)
    p3 = np.zeros((320, 8 * BLK), np.float32)
    p4 = np.zeros((64, 8 * BLK), np.float32)
    p5 = np.zeros((320, 128), np.float32)
    m5 = np.zeros((320, 128), np.float32)
    for h in range(2):
        for x in range(4):
            for z in range(8):
                j = h * 4 + x
                p2[x * 96 + 80 + h * 8 + z, z * BLK + 40 + j] = 1
                p4[h * 32 + z * 4 + x, x * 96 + 80 + h * 8 + z] = 1
                for s in range(CAP):
                    p2[x * 96 + h * 40 + z * CAP + s, z * BLK + j * CAP + s] = 1
                    p3[h * 160 + z * 20 + x * CAP + s, x * 96 + h * 40 + z * CAP + s] = 1
                    row = z * 40 + j * CAP + s
                    p5[row, h * 32 + z * 4 + x] = 1
                    m5[row, s] = 1
    return p2, p3, p4, p5, m5


def kernel(
    rw, grad_in, gate_in, up_in, wd_in, wg_in, wu_in, routes_in, ed_in, hid_in,
    p2_in, p3_in, p4_in, p5_in, m5_in,
    out_g, out_h, out_r,
    gate, up, routes, hid, p2, p3, p4, p5, m5,
    W, G, SL, S1, R1, S2, R2, DB, WR, WX, ED, half_acc, acc, K, XS, XR, YS, YR, RT0, RT1, ST2, RT2,
    ssem, rsem, lsem, xsend, xrecv, ysend, yrecv,
):
    e = lax.axis_index("expert")
    t = lax.axis_index("tensor")
    z = e // 8
    j = lax.rem(e, 8)
    yh = j // 4
    x = lax.rem(j, 4)
    yl = t // 2
    c = lax.rem(t, 2)
    yo = 1 - yh

    def zz(d):
        return lax.rem(z + d + 8, 8)

    def xx(d):
        return lax.rem(x + d, 4)

    def z_dev(d):
        return (zz(d) * 8 + j, t)

    def x_dev(d):
        return (z * 8 + yh * 4 + xx(d), t)

    def j_dev(d):
        return (z * 8 + lax.rem(j + d, 8), t)

    y_dev = (z * 8 + yo * 4 + x, t)
    sibling = (e, yl * 2 + 1 - c)

    def yl_dev(d):
        return (e, lax.rem(yl + d, 4) * 2 + c)

    def t_dev(d):
        return (e, lax.rem(t + d, 8))

    def far_dev(d):
        return (z * 8 + yo * 4 + x, lax.rem(yl + d, 4) * 2 + c)

    barrier = pltpu.get_barrier_semaphore()
    for d in range(1, 8):
        for dev in (z_dev(d), j_dev(d), t_dev(d)):
            pl.semaphore_signal(barrier, inc=1, device_id=dev, device_id_type=MESH)
    for d in range(1, 4):
        pl.semaphore_signal(barrier, inc=1, device_id=far_dev(d), device_id_type=MESH)

    local = {}

    def fetch(name, src, dst):
        copy = pltpu.make_async_copy(src, dst, lsem.at[len(local)])
        copy.start()
        local[name] = copy

    fetch("wd", wd_in, W.at[0, z, yh, x])
    fetch("wg", wg_in, W.at[1, z, yh, x])
    fetch("wu", wu_in, W.at[2, z, yh, x])
    fetch("grad", grad_in, G.at[t])
    fetch("routes", routes_in, routes)
    fetch("p2", p2_in, p2)
    fetch("p3", p3_in, p3)
    fetch("p4", p4_in, p4)
    fetch("p5", p5_in, p5)
    fetch("m5", m5_in, m5)
    fetch("gate", gate_in, gate)
    fetch("up", up_in, up)
    fetch("hid", hid_in, hid)
    fetch("ed", ed_in, ED)

    count = [0]
    sends = []

    def send(src, dst, dev):
        i = count[0]
        count[0] += 1
        copy = pltpu.make_async_remote_copy(
            src_ref=src, dst_ref=dst, send_sem=ssem.at[i], recv_sem=rsem.at[i],
            device_id=dev, device_id_type=MESH,
        )
        copy.start()
        sends.append(copy)
        return copy

    kinds = (pl.ds(0, 1), pl.ds(1, 2))

    def ring(key, step, right):
        sign = 1 if right else -1
        zc = zz(-sign * (step - 1))
        if key == "own":
            ref = W.at[kinds[1], zc, yh]
            if step == 4:
                ref = W.at[kinds[1], zc, yh, pl.ds(0 if right else 2, 2)]
        else:
            kd, far_half = key
            half = yo if far_half else yh
            ref = W.at[kinds[kd], zc, half, x]
            if step == 4:
                ref = W.at[kinds[kd], zc, half, x, pl.ds(0 if right else 32, 32)]
        return send(ref, ref, z_dev(sign))

    def x_send(key, delta):
        kd, far_half = key
        ref = W.at[kinds[kd], zz(delta), yo if far_half else yh, x]
        return [send(ref, ref, x_dev(1)), send(ref, ref, x_dev(3))]

    def x_relay(key, delta):
        kd, far_half = key
        block = W.at[kinds[kd], zz(delta), yo if far_half else yh]
        ax[key, delta][0].wait_recv()
        low = block.at[:, xx(3), pl.ds(0, 32)]
        relay = [send(low, low, x_dev(1))]
        ax[key, delta][1].wait_recv()
        high = block.at[:, xx(1), pl.ds(32, 32)]
        relay.append(send(high, high, x_dev(3)))
        ar[key, delta] = relay

    def gather_start(buf):
        own = buf.at[t]
        return [send(own, own, yl_dev(d)) for d in range(1, 4)] + [send(own, own, sibling)]

    def gather_forward(buf, first_copies):
        out = []
        for d in range(1, 4):
            first_copies[d - 1].wait_recv()
            ref = buf.at[lax.rem(yl - d + 4, 4) * 2 + c]
            out.append(send(ref, ref, sibling))
        return out

    a = {}
    b = {}
    ax = {}
    ar = {}
    down_own, down_far, wide_far = (0, False), (0, True), (1, True)

    def a_open(key):
        if key[1]:
            across[key[0]].wait_recv()
        for right in (True, False):
            a[key, 1, right] = ring(key, 1, right)
        ax[key, 0] = x_send(key, 0)

    def a_step(key, step):
        a[key, step, True].wait_recv()
        if step < 4:
            a[key, step + 1, True] = ring(key, step + 1, True)
        a[key, step, False].wait_recv()
        if step < 4:
            a[key, step + 1, False] = ring(key, step + 1, False)
            ax[key, -step] = x_send(key, -step)
            ax[key, step] = x_send(key, step)
        else:
            ax[key, 4] = x_send(key, 4)

    def relay_step(key, step):
        if step in (0, 4):
            x_relay(key, step)
        else:
            x_relay(key, -step)
            x_relay(key, step)

    def b_open():
        for copy in bx:
            copy.wait_recv()
        for right in (True, False):
            b[1, right] = ring("own", 1, right)

    def b_step(step):
        b[step, True].wait_recv()
        if step < 4:
            b[step + 1, True] = ring("own", step + 1, True)
        b[step, False].wait_recv()
        if step < 4:
            b[step + 1, False] = ring("own", step + 1, False)

    lane = lax.broadcasted_iota(jnp.int32, (128, 128), 1).astype(F32)
    row = lax.broadcasted_iota(jnp.int32, (128, 128), 0).astype(F32)
    lane_b = lax.broadcasted_iota(jnp.int32, (128, 8 * BLK), 1).astype(F32)
    local["routes"].wait()

    def column(values):
        return jnp.sum(jnp.where(lane == row, values, 0.0), axis=1, keepdims=True)

    high = [lax.shift_right_logical(routes[k : k + 1, :], 3) for k in range(2)]
    low = [lax.bitwise_and(routes[k : k + 1, :], 7) for k in range(2)]
    base = [column((high[k] * BLK + low[k] * CAP).astype(F32)) for k in range(2)]
    spare = [column((high[k] * BLK + low[k] + 40).astype(F32)) for k in range(2)]
    onehot = [(column(routes[k : k + 1, :].astype(F32)) == lane).astype(F32) for k in range(2)]
    lower = (lane < row).astype(BF16)
    earlier = dot_nn(lower, (onehot[0] + onehot[1]).astype(BF16))
    rank = [
        jnp.sum(earlier * onehot[0], axis=1, keepdims=True),
        jnp.sum((earlier + onehot[0]) * onehot[1], axis=1, keepdims=True),
    ]
    slot_map = jnp.zeros((128, 8 * BLK), F32)
    weight_rows = jnp.zeros((8 * BLK, 128), F32)
    for k in range(2):
        slot_map += (base[k] + rank[k] == lane_b).astype(F32)
        weight = column(rw[k : k + 1, :].astype(F32))
        value = jnp.where(lane == rank[k], weight, 0.0).astype(BF16)
        weight_rows += dot_tn((spare[k] == lane_b).astype(BF16), value)
    local["grad"].wait()
    filled = dot_tn(slot_map.astype(BF16), G[t])
    first = (filled[:, 0:128] + weight_rows).astype(BF16)
    for k in range(8):
        S1[k, :, 0:128] = first[k * BLK : (k + 1) * BLK]
        S1[k, :, 128:512] = filled[k * BLK : (k + 1) * BLK, 128:512].astype(BF16)
    R1[z] = S1[z]

    pl.semaphore_wait(barrier, 24)
    local["wd"].wait()
    local["wg"].wait()
    local["wu"].wait()
    a_open(down_own)
    ref = W.at[kinds[1], z, yh, x]
    bx = [send(ref, ref, x_dev(d)) for d in range(1, 4)]
    across = []
    for kd in range(2):
        ref = W.at[kinds[kd], z, yh, x]
        across.append(send(ref, ref, y_dev))
    disp1 = [send(S1.at[zz(d)], R1.at[z], z_dev(d)) for d in range(1, 8)]
    tok = gather_start(G)
    local["p2"].wait()
    for copy in disp1:
        copy.wait_recv()
    shuffled = dot_nn(p2[...], R1[...].reshape(8 * BLK, 512)).astype(BF16)
    S2[...] = shuffled.reshape(4, 96, 512)
    R2[x] = S2[x]
    disp2 = [send(S2.at[xx(d)], R2.at[x], x_dev(d)) for d in range(1, 4)]
    a_step(down_own, 1)
    b_open()
    a_open(down_far)
    a_open(wide_far)
    a_step(down_own, 2)
    tok_fwd = gather_forward(G, tok)

    for name in ("p3", "p4", "p5", "m5"):
        local[name].wait()
    for copy in disp2:
        copy.wait_recv()
    arrived = R2[...].reshape(8 * BLK, 512)
    DB[...] = dot_nn(p3[...], arrived).astype(BF16).reshape(2, 160, 512)
    WR[...] = dot_nn(p4[...], arrived[:, 0:128]).astype(BF16).reshape(2, 32, 128)
    SL[yh, t] = DB[yh]
    mine = SL.at[yh, t]
    near = [send(mine, mine, yl_dev(d)) for d in range(1, 4)]
    far = [send(DB.at[yo], mine, far_dev(d)) for d in range(4)]
    twin = [send(mine, mine, sibling)]
    weights_far = send(WR.at[yo], WX, y_dev)
    sends.pop()

    a_step(down_far, 1)
    a_step(wide_far, 1)
    a_step(down_own, 3)
    a_step(down_far, 2)
    a_step(down_own, 4)
    relay_step(down_own, 0)
    b_step(1)
    a_step(wide_far, 2)
    relay_step(down_own, 1)
    relay_step(down_far, 0)
    a_step(down_far, 3)
    relay_step(wide_far, 0)
    relay_step(down_own, 2)
    relay_step(down_far, 1)
    a_step(wide_far, 3)
    a_step(down_far, 4)
    b_step(2)
    relay_step(down_own, 3)
    relay_step(wide_far, 1)
    relay_step(down_far, 2)
    a_step(wide_far, 4)
    for name in ("hid", "ed"):
        local[name].wait()
    def expert_term(h, idx):
        cols = pl.ds(pl.multiple_of(idx * 512, 512), 512)
        return dot_nt(SL[h, idx], ED[:, cols])

    half_acc[yh] = expert_term(yh, t)
    for d in range(1, 4):
        near[d - 1].wait_recv()
        idx = lax.rem(yl - d + 4, 4) * 2 + c
        twin.append(send(SL.at[yh, idx], SL.at[yh, idx], sibling))
        half_acc[yh] += expert_term(yh, idx)
    for d in range(4):
        far[d].wait_recv()
        idx = lax.rem(yl - d + 4, 4) * 2 + c
        twin.append(send(SL.at[yo, idx], SL.at[yo, idx], sibling))
        if d == 0:
            half_acc[yo] = expert_term(yo, idx)
        else:
            half_acc[yo] += expert_term(yo, idx)
    for d in range(4):
        twin[d].wait_recv()
        half_acc[yh] += expert_term(yh, lax.rem(yl - d + 4, 4) * 2 + 1 - c)
    for d in range(4):
        twin[4 + d].wait_recv()
        half_acc[yo] += expert_term(yo, lax.rem(yl - d + 4, 4) * 2 + 1 - c)
    for h in range(2):
        for k in range(8):
            acc[k * 40 + h * 20 : k * 40 + h * 20 + 20, :] = half_acc[h, k * 20 : k * 20 + 20, :]
    weights_far.wait()
    WR[yo] = WX[...]
    all_weights = jnp.concatenate(
        [WR[...].reshape(64, 128), jnp.zeros((64, 128), BF16)], axis=0
    )
    slot_weight = jnp.sum(dot_nn(p5[...], all_weights) * m5[...], axis=1, keepdims=True)
    out_h[...] = (slot_weight * acc[...]).astype(BF16)
    products = jnp.sum(hid[...].astype(F32) * acc[...], axis=1, keepdims=True)
    diag = lax.broadcasted_iota(jnp.int32, (40, 128), 0) == lax.broadcasted_iota(
        jnp.int32, (40, 128), 1
    )
    tile = jnp.concatenate(
        [
            jnp.sum(jnp.where(diag, products[k * 40 : (k + 1) * 40], 0.0), axis=0, keepdims=True)
            for k in range(8)
        ],
        axis=0,
    )
    RT0[t] = tile
    own = RT0.at[t]
    ret0 = [send(own, own, t_dev(d)) for d in range(1, 8)]

    relay_step(down_own, 4)
    relay_step(down_far, 3)
    for copy in ret0:
        copy.wait_recv()
    RT1[j] = jnp.sum(RT0[...], axis=0)
    own1 = RT1.at[j]
    ret1 = [send(own1, own1, j_dev(d)) for d in range(1, 8)]
    relay_step(wide_far, 2)
    relay_step(down_far, 4)
    relay_step(wide_far, 3)
    for copy in ret1:
        copy.wait_recv()
    for k in range(8):
        ST2[k] = RT1[:, k, :]
    RT2[z] = ST2[z]
    ret2 = [send(ST2.at[zz(d)], RT2.at[z], z_dev(d)) for d in range(1, 8)]
    x_relay(wide_far, 4)
    b_step(3)

    tok[3].wait_recv()
    for copy in tok_fwd:
        copy.wait_recv()
    for delta in (0, -1, 1, -2, 2, -3, 3, 4):
        for copy in ar[down_own, delta] + ar[down_far, delta]:
            copy.wait_recv()
    for name in ("gate", "up"):
        local[name].wait()
    hd = jnp.zeros((128, 384), F32)
    for k in range(8):
        hd += dot_nn(G[k], W[0, k].reshape(512, 384))
    gate_f = gate[...].astype(F32)
    up_f = up[...].astype(F32)
    sig = jax.nn.sigmoid(gate_f)
    swish = gate_f * sig
    slope = sig * (1.0 + gate_f * (1.0 - sig))
    gd = (hd * up_f * slope).astype(BF16)
    ud = (hd * swish).astype(BF16)

    def sib_copy(zb):
        return pltpu.make_async_remote_copy(
            src_ref=XS.at[zb], dst_ref=XR.at[zb], send_sem=xsend.at[zb], recv_sem=xrecv.at[zb],
            device_id=sibling, device_id_type=MESH,
        )

    def y_copy(zb, src):
        return pltpu.make_async_remote_copy(
            src_ref=YS.at[zb], dst_ref=YR.at[src], send_sem=ysend.at[zb], recv_sem=yrecv.at[src],
            device_id=(e, zb), device_id_type=MESH,
        )

    def part(delta):
        zb = zz(delta)
        for copy in ar[wide_far, delta]:
            copy.wait_recv()
        value = dot_nt(gd, W[1, zb].reshape(512, 384)) + dot_nt(ud, W[2, zb].reshape(512, 384))

        @pl.when(lax.rem(zb, 2) == c)
        def _():
            K[zb] = value

        @pl.when(lax.rem(zb, 2) != c)
        def _():
            XS[zb] = value.astype(BF16)
            sib_copy(zb).start()

    def pass_on(delta):
        zb = zz(delta)

        @pl.when(lax.rem(zb, 2) == c)
        def _():
            sib_copy(zb).wait_recv()
            K[zb] = K[zb] + XR[zb].astype(F32)

            @pl.when(zb != t)
            def _():
                YS[zb] = K[zb].astype(BF16)
                y_copy(zb, yl).start()

    part(0)
    part(-1)
    pass_on(0)
    part(1)
    pass_on(-1)
    pass_on(1)
    part(-2)
    part(2)
    pass_on(-2)
    pass_on(2)
    for copy in ret2:
        copy.wait_recv()
    back = RT2[...].reshape(64, 128)
    jf = (j * CAP).astype(F32)
    for k in range(2):
        scores = jnp.dot(
            onehot[k][:, 0:64], back, preferred_element_type=F32, precision=lax.Precision.HIGHEST
        )
        score = jnp.sum(jnp.where(lane == rank[k] + jf, scores, 0.0), axis=1, keepdims=True)
        out_r[k : k + 1, :] = jnp.sum(jnp.where(lane == row, score, 0.0), axis=0, keepdims=True)

    part(-3)
    part(3)
    pass_on(-3)
    b_step(4)
    pass_on(3)
    part(4)
    pass_on(4)
    total = K[t]
    for d in range(1, 4):
        src = lax.rem(yl + d, 4)
        y_copy(t, src).wait_recv()
        total += YR[src].astype(F32)
    out_g[...] = total.astype(BF16)
    for d in range(1, 4):
        y_copy(lax.rem(yl + d, 4) * 2 + c, yl).wait_send()
    for q in range(4):
        sib_copy(q * 2 + 1 - c).wait_send()
    for copy in sends:
        copy.wait_send()


def body(
    grad_out, dense_gate, dense_up, w_gate, w_up, w_down, routes, route_weight,
    expert_down, expert_hidden,
):
    p2, p3, p4, p5, m5 = tables()
    vmem = pl.BlockSpec(memory_space=pltpu.VMEM)
    hbm = pl.BlockSpec(memory_space=pltpu.HBM)
    out_g, out_h, out_r = pl.pallas_call(
        kernel,
        out_shape=(
            jax.ShapeDtypeStruct((128, 512), BF16),
            jax.ShapeDtypeStruct((320, 384), BF16),
            jax.ShapeDtypeStruct((2, 128), F32),
        ),
        in_specs=[vmem] + [hbm] * 14,
        out_specs=(vmem, vmem, vmem),
        scratch_shapes=[
            pltpu.VMEM((128, 384), BF16),
            pltpu.VMEM((128, 384), BF16),
            pltpu.VMEM((2, 128), jnp.int32),
            pltpu.VMEM((320, 384), BF16),
            pltpu.VMEM((8 * BLK, 8 * BLK), BF16),
            pltpu.VMEM((320, 8 * BLK), BF16),
            pltpu.VMEM((64, 8 * BLK), BF16),
            pltpu.VMEM((320, 128), BF16),
            pltpu.VMEM((320, 128), F32),
            pltpu.VMEM((3, 8, 2, 4, 64, 384), BF16),
            pltpu.VMEM((8, 128, 512), BF16),
            pltpu.VMEM((2, 8, 160, 512), BF16),
            pltpu.VMEM((8, BLK, 512), BF16),
            pltpu.VMEM((8, BLK, 512), BF16),
            pltpu.VMEM((4, 96, 512), BF16),
            pltpu.VMEM((4, 96, 512), BF16),
            pltpu.VMEM((2, 160, 512), BF16),
            pltpu.VMEM((2, 32, 128), BF16),
            pltpu.VMEM((32, 128), BF16),
            pltpu.VMEM((384, 4096), BF16),
            pltpu.VMEM((2, 160, 384), F32),
            pltpu.VMEM((320, 384), F32),
            pltpu.VMEM((8, 128, 512), F32),
            pltpu.VMEM((8, 128, 512), BF16),
            pltpu.VMEM((8, 128, 512), BF16),
            pltpu.VMEM((8, 128, 512), BF16),
            pltpu.VMEM((4, 128, 512), BF16),
            pltpu.VMEM((8, 8, 128), F32),
            pltpu.VMEM((8, 8, 128), F32),
            pltpu.VMEM((8, 8, 128), F32),
            pltpu.VMEM((8, 8, 128), F32),
            pltpu.SemaphoreType.DMA((N_COPY,)),
            pltpu.SemaphoreType.DMA((N_COPY,)),
            pltpu.SemaphoreType.DMA((16,)),
            pltpu.SemaphoreType.DMA((8,)),
            pltpu.SemaphoreType.DMA((8,)),
            pltpu.SemaphoreType.DMA((8,)),
            pltpu.SemaphoreType.DMA((4,)),
        ],
        compiler_params=pltpu.CompilerParams(
            collective_id=0, has_side_effects=True, vmem_limit_bytes=60 << 20
        ),
    )(
        route_weight.T, grad_out, dense_gate, dense_up, w_down.T, w_gate, w_up, routes.T,
        expert_down[0], expert_hidden[0],
        jnp.asarray(p2, BF16), jnp.asarray(p3, BF16), jnp.asarray(p4, BF16), jnp.asarray(p5, BF16),
        jnp.asarray(m5, F32),
    )
    return out_g, out_h[None], out_r.T


def solution(mesh):
    in_specs = (
        P("expert", "tensor"),
        P("expert", "tensor"),
        P("expert", "tensor"),
        P("expert", "tensor"),
        P("expert", "tensor"),
        P("tensor", "expert"),
        P("expert", None),
        P("expert", None),
        P("expert", "tensor", None),
        P("expert", None, "tensor"),
    )
    out_specs = (P("expert", "tensor"), P("expert", None, "tensor"), P("expert", None))
    return jax.shard_map(body, mesh=mesh, in_specs=in_specs, out_specs=out_specs, check_vma=False)
```

```python
import jax
import jax.numpy as jnp
import numpy as np
from jax import lax
from jax.experimental import pallas as pl
from jax.experimental.pallas import tpu as pltpu
from jax.sharding import PartitionSpec as P

MESH = pl.DeviceIdType.MESH
F32 = jnp.float32
BF16 = jnp.bfloat16
CAP = 5
BLK = 48
N_COPY = 224


def dot_nt(a, b):
    return lax.dot_general(a, b, (((1,), (1,)), ((), ())), preferred_element_type=F32)


def dot_tn(a, b):
    return lax.dot_general(a, b, (((0,), (0,)), ((), ())), preferred_element_type=F32)


def dot_nn(a, b):
    return jnp.dot(a, b, preferred_element_type=F32)


def tables():
    p2 = np.zeros((8 * BLK, 8 * BLK), np.float32)
    p3 = np.zeros((320, 8 * BLK), np.float32)
    p4 = np.zeros((64, 8 * BLK), np.float32)
    p5 = np.zeros((320, 128), np.float32)
    m5 = np.zeros((320, 128), np.float32)
    for h in range(2):
        for x in range(4):
            for z in range(8):
                j = h * 4 + x
                p2[x * 96 + 80 + h * 8 + z, z * BLK + 40 + j] = 1
                p4[h * 32 + z * 4 + x, x * 96 + 80 + h * 8 + z] = 1
                for s in range(CAP):
                    p2[x * 96 + h * 40 + z * CAP + s, z * BLK + j * CAP + s] = 1
                    p3[h * 160 + z * 20 + x * CAP + s, x * 96 + h * 40 + z * CAP + s] = 1
                    row = z * 40 + j * CAP + s
                    p5[row, h * 32 + z * 4 + x] = 1
                    m5[row, s] = 1
    return p2, p3, p4, p5, m5


def kernel(
    rw, grad_in, gate_in, up_in, wd_in, wg_in, wu_in, routes_in, ed_in, hid_in,
    p2_in, p3_in, p4_in, p5_in, m5_in,
    out_g, out_h, out_r,
    gate, up, routes, hid, p2, p3, p4, p5, m5,
    W, G, SL, S1, R1, S2, R2, DB, WR, WX, ED, half_acc, acc, K, XS, XR, YS, YR, RT0, RT1, ST2, RT2,
    ssem, rsem, lsem, xsend, xrecv, ysend, yrecv,
):
    e = lax.axis_index("expert")
    t = lax.axis_index("tensor")
    z = e // 8
    j = lax.rem(e, 8)
    yh = j // 4
    x = lax.rem(j, 4)
    yl = t // 2
    c = lax.rem(t, 2)
    yo = 1 - yh

    def zz(d):
        return lax.rem(z + d + 8, 8)

    def xx(d):
        return lax.rem(x + d, 4)

    def z_dev(d):
        return (zz(d) * 8 + j, t)

    def x_dev(d):
        return (z * 8 + yh * 4 + xx(d), t)

    def j_dev(d):
        return (z * 8 + lax.rem(j + d, 8), t)

    y_dev = (z * 8 + yo * 4 + x, t)
    sibling = (e, yl * 2 + 1 - c)

    def yl_dev(d):
        return (e, lax.rem(yl + d, 4) * 2 + c)

    def t_dev(d):
        return (e, lax.rem(t + d, 8))

    def far_dev(d):
        return (z * 8 + yo * 4 + x, lax.rem(yl + d, 4) * 2 + c)

    barrier = pltpu.get_barrier_semaphore()
    for d in range(1, 8):
        for dev in (z_dev(d), j_dev(d), t_dev(d)):
            pl.semaphore_signal(barrier, inc=1, device_id=dev, device_id_type=MESH)
    for d in range(1, 4):
        pl.semaphore_signal(barrier, inc=1, device_id=far_dev(d), device_id_type=MESH)

    local = {}

    def fetch(name, src, dst):
        copy = pltpu.make_async_copy(src, dst, lsem.at[len(local)])
        copy.start()
        local[name] = copy

    fetch("wd", wd_in, W.at[0, z, yh, x])
    fetch("wg", wg_in, W.at[1, z, yh, x])
    fetch("wu", wu_in, W.at[2, z, yh, x])
    fetch("grad", grad_in, G.at[t])
    fetch("routes", routes_in, routes)
    fetch("p2", p2_in, p2)
    fetch("p3", p3_in, p3)
    fetch("p4", p4_in, p4)
    fetch("p5", p5_in, p5)
    fetch("m5", m5_in, m5)
    fetch("gate", gate_in, gate)
    fetch("up", up_in, up)
    fetch("hid", hid_in, hid)
    fetch("ed", ed_in, ED)

    count = [0]
    sends = []

    def send(src, dst, dev):
        i = count[0]
        count[0] += 1
        copy = pltpu.make_async_remote_copy(
            src_ref=src, dst_ref=dst, send_sem=ssem.at[i], recv_sem=rsem.at[i],
            device_id=dev, device_id_type=MESH,
        )
        copy.start()
        sends.append(copy)
        return copy

    kinds = (pl.ds(0, 1), pl.ds(1, 2))

    def ring(key, step, right):
        sign = 1 if right else -1
        zc = zz(-sign * (step - 1))
        if key == "own":
            ref = W.at[kinds[1], zc, yh]
            if step == 4:
                ref = W.at[kinds[1], zc, yh, pl.ds(0 if right else 2, 2)]
        else:
            kd, far_half = key
            half = yo if far_half else yh
            ref = W.at[kinds[kd], zc, half, x]
            if step == 4:
                ref = W.at[kinds[kd], zc, half, x, pl.ds(0 if right else 32, 32)]
        return send(ref, ref, z_dev(sign))

    def x_send(key, delta):
        kd, far_half = key
        ref = W.at[kinds[kd], zz(delta), yo if far_half else yh, x]
        return [send(ref, ref, x_dev(1)), send(ref, ref, x_dev(3))]

    def x_relay(key, delta):
        kd, far_half = key
        block = W.at[kinds[kd], zz(delta), yo if far_half else yh]
        ax[key, delta][0].wait_recv()
        low = block.at[:, xx(3), pl.ds(0, 32)]
        relay = [send(low, low, x_dev(1))]
        ax[key, delta][1].wait_recv()
        high = block.at[:, xx(1), pl.ds(32, 32)]
        relay.append(send(high, high, x_dev(3)))
        ar[key, delta] = relay

    def gather_start(buf):
        own = buf.at[t]
        return [send(own, own, yl_dev(d)) for d in range(1, 4)] + [send(own, own, sibling)]

    def gather_forward(buf, first_copies):
        out = []
        for d in range(1, 4):
            first_copies[d - 1].wait_recv()
            ref = buf.at[lax.rem(yl - d + 4, 4) * 2 + c]
            out.append(send(ref, ref, sibling))
        return out

    a = {}
    b = {}
    ax = {}
    ar = {}
    down_own, down_far, wide_far = (0, False), (0, True), (1, True)

    def a_open(key):
        if key[1]:
            across[key[0]].wait_recv()
        for right in (True, False):
            a[key, 1, right] = ring(key, 1, right)
        ax[key, 0] = x_send(key, 0)

    def a_step(key, step):
        a[key, step, True].wait_recv()
        if step < 4:
            a[key, step + 1, True] = ring(key, step + 1, True)
        a[key, step, False].wait_recv()
        if step < 4:
            a[key, step + 1, False] = ring(key, step + 1, False)
            ax[key, -step] = x_send(key, -step)
            ax[key, step] = x_send(key, step)
        else:
            ax[key, 4] = x_send(key, 4)

    def relay_step(key, step):
        if step in (0, 4):
            x_relay(key, step)
        else:
            x_relay(key, -step)
            x_relay(key, step)

    def b_open():
        for copy in bx:
            copy.wait_recv()
        for right in (True, False):
            b[1, right] = ring("own", 1, right)

    def b_step(step):
        b[step, True].wait_recv()
        if step < 4:
            b[step + 1, True] = ring("own", step + 1, True)
        b[step, False].wait_recv()
        if step < 4:
            b[step + 1, False] = ring("own", step + 1, False)

    lane = lax.broadcasted_iota(jnp.int32, (128, 128), 1).astype(F32)
    row = lax.broadcasted_iota(jnp.int32, (128, 128), 0).astype(F32)
    lane_b = lax.broadcasted_iota(jnp.int32, (128, 8 * BLK), 1).astype(F32)
    local["routes"].wait()

    def column(values):
        return jnp.sum(jnp.where(lane == row, values, 0.0), axis=1, keepdims=True)

    high = [lax.shift_right_logical(routes[k : k + 1, :], 3) for k in range(2)]
    low = [lax.bitwise_and(routes[k : k + 1, :], 7) for k in range(2)]
    base = [column((high[k] * BLK + low[k] * CAP).astype(F32)) for k in range(2)]
    spare = [column((high[k] * BLK + low[k] + 40).astype(F32)) for k in range(2)]
    onehot = [(column(routes[k : k + 1, :].astype(F32)) == lane).astype(F32) for k in range(2)]
    lower = (lane < row).astype(BF16)
    earlier = dot_nn(lower, (onehot[0] + onehot[1]).astype(BF16))
    rank = [
        jnp.sum(earlier * onehot[0], axis=1, keepdims=True),
        jnp.sum((earlier + onehot[0]) * onehot[1], axis=1, keepdims=True),
    ]
    slot_map = jnp.zeros((128, 8 * BLK), F32)
    weight_rows = jnp.zeros((8 * BLK, 128), F32)
    for k in range(2):
        slot_map += (base[k] + rank[k] == lane_b).astype(F32)
        weight = column(rw[k : k + 1, :].astype(F32))
        value = jnp.where(lane == rank[k], weight, 0.0).astype(BF16)
        weight_rows += dot_tn((spare[k] == lane_b).astype(BF16), value)
    local["grad"].wait()
    filled = dot_tn(slot_map.astype(BF16), G[t])
    first = (filled[:, 0:128] + weight_rows).astype(BF16)
    for k in range(8):
        S1[k, :, 0:128] = first[k * BLK : (k + 1) * BLK]
        S1[k, :, 128:512] = filled[k * BLK : (k + 1) * BLK, 128:512].astype(BF16)
    R1[z] = S1[z]

    pl.semaphore_wait(barrier, 24)
    local["wd"].wait()
    local["wg"].wait()
    local["wu"].wait()
    a_open(down_own)
    ref = W.at[kinds[1], z, yh, x]
    bx = [send(ref, ref, x_dev(d)) for d in range(1, 4)]
    across = []
    for kd in range(2):
        ref = W.at[kinds[kd], z, yh, x]
        across.append(send(ref, ref, y_dev))
    disp1 = [send(S1.at[zz(d)], R1.at[z], z_dev(d)) for d in range(1, 8)]
    tok = gather_start(G)
    local["p2"].wait()
    for copy in disp1:
        copy.wait_recv()
    shuffled = dot_nn(p2[...], R1[...].reshape(8 * BLK, 512)).astype(BF16)
    S2[...] = shuffled.reshape(4, 96, 512)
    R2[x] = S2[x]
    disp2 = [send(S2.at[xx(d)], R2.at[x], x_dev(d)) for d in range(1, 4)]
    a_step(down_own, 1)
    b_open()
    a_open(down_far)
    a_open(wide_far)
    a_step(down_own, 2)
    tok_fwd = gather_forward(G, tok)

    for name in ("p3", "p4", "p5", "m5"):
        local[name].wait()
    for copy in disp2:
        copy.wait_recv()
    arrived = R2[...].reshape(8 * BLK, 512)
    DB[...] = dot_nn(p3[...], arrived).astype(BF16).reshape(2, 160, 512)
    WR[...] = dot_nn(p4[...], arrived[:, 0:128]).astype(BF16).reshape(2, 32, 128)
    SL[yh, t] = DB[yh]
    mine = SL.at[yh, t]
    near = [send(mine, mine, yl_dev(d)) for d in range(1, 4)]
    far = [send(DB.at[yo], mine, far_dev(d)) for d in range(4)]
    twin = [send(mine, mine, sibling)]
    weights_far = send(WR.at[yo], WX, y_dev)
    sends.pop()

    a_step(down_far, 1)
    a_step(wide_far, 1)
    a_step(down_own, 3)
    a_step(down_far, 2)
    a_step(down_own, 4)
    relay_step(down_own, 0)
    b_step(1)
    a_step(wide_far, 2)
    relay_step(down_own, 1)
    relay_step(down_far, 0)
    a_step(down_far, 3)
    relay_step(wide_far, 0)
    relay_step(down_own, 2)
    relay_step(down_far, 1)
    a_step(wide_far, 3)
    a_step(down_far, 4)
    b_step(2)
    relay_step(down_own, 3)
    relay_step(wide_far, 1)
    relay_step(down_far, 2)

    for name in ("hid", "ed"):
        local[name].wait()
    def expert_term(h, idx):
        cols = pl.ds(pl.multiple_of(idx * 512, 512), 512)
        return dot_nt(SL[h, idx], ED[:, cols])

    half_acc[yh] = expert_term(yh, t)
    for d in range(1, 4):
        near[d - 1].wait_recv()
        idx = lax.rem(yl - d + 4, 4) * 2 + c
        twin.append(send(SL.at[yh, idx], SL.at[yh, idx], sibling))
        half_acc[yh] += expert_term(yh, idx)
    for d in range(4):
        far[d].wait_recv()
        idx = lax.rem(yl - d + 4, 4) * 2 + c
        twin.append(send(SL.at[yo, idx], SL.at[yo, idx], sibling))
        if d == 0:
            half_acc[yo] = expert_term(yo, idx)
        else:
            half_acc[yo] += expert_term(yo, idx)
    for d in range(4):
        twin[d].wait_recv()
        half_acc[yh] += expert_term(yh, lax.rem(yl - d + 4, 4) * 2 + 1 - c)
    for d in range(4):
        twin[4 + d].wait_recv()
        half_acc[yo] += expert_term(yo, lax.rem(yl - d + 4, 4) * 2 + 1 - c)
    for h in range(2):
        for k in range(8):
            acc[k * 40 + h * 20 : k * 40 + h * 20 + 20, :] = half_acc[h, k * 20 : k * 20 + 20, :]
    weights_far.wait()
    WR[yo] = WX[...]
    all_weights = jnp.concatenate(
        [WR[...].reshape(64, 128), jnp.zeros((64, 128), BF16)], axis=0
    )
    slot_weight = jnp.sum(dot_nn(p5[...], all_weights) * m5[...], axis=1, keepdims=True)
    out_h[...] = (slot_weight * acc[...]).astype(BF16)
    products = jnp.sum(hid[...].astype(F32) * acc[...], axis=1, keepdims=True)
    diag = lax.broadcasted_iota(jnp.int32, (40, 128), 0) == lax.broadcasted_iota(
        jnp.int32, (40, 128), 1
    )
    tile = jnp.concatenate(
        [
            jnp.sum(jnp.where(diag, products[k * 40 : (k + 1) * 40], 0.0), axis=0, keepdims=True)
            for k in range(8)
        ],
        axis=0,
    )
    RT0[t] = tile
    own = RT0.at[t]
    ret0 = [send(own, own, t_dev(d)) for d in range(1, 8)]

    a_step(wide_far, 4)

    relay_step(down_own, 4)
    relay_step(down_far, 3)
    for copy in ret0:
        copy.wait_recv()
    RT1[j] = jnp.sum(RT0[...], axis=0)
    own1 = RT1.at[j]
    ret1 = [send(own1, own1, j_dev(d)) for d in range(1, 8)]
    relay_step(wide_far, 2)
    relay_step(down_far, 4)
    relay_step(wide_far, 3)
    for copy in ret1:
        copy.wait_recv()
    for k in range(8):
        ST2[k] = RT1[:, k, :]
    RT2[z] = ST2[z]
    ret2 = [send(ST2.at[zz(d)], RT2.at[z], z_dev(d)) for d in range(1, 8)]
    x_relay(wide_far, 4)
    b_step(3)

    tok[3].wait_recv()
    for copy in tok_fwd:
        copy.wait_recv()
    for delta in (0, -1, 1, -2, 2, -3, 3, 4):
        for copy in ar[down_own, delta] + ar[down_far, delta]:
            copy.wait_recv()
    for name in ("gate", "up"):
        local[name].wait()
    hd = jnp.zeros((128, 384), F32)
    for k in range(8):
        hd += dot_nn(G[k], W[0, k].reshape(512, 384))
    gate_f = gate[...].astype(F32)
    up_f = up[...].astype(F32)
    sig = jax.nn.sigmoid(gate_f)
    swish = gate_f * sig
    slope = sig * (1.0 + gate_f * (1.0 - sig))
    gd = (hd * up_f * slope).astype(BF16)
    ud = (hd * swish).astype(BF16)

    def sib_copy(zb):
        return pltpu.make_async_remote_copy(
            src_ref=XS.at[zb], dst_ref=XR.at[zb], send_sem=xsend.at[zb], recv_sem=xrecv.at[zb],
            device_id=sibling, device_id_type=MESH,
        )

    def y_copy(zb, src):
        return pltpu.make_async_remote_copy(
            src_ref=YS.at[zb], dst_ref=YR.at[src], send_sem=ysend.at[zb], recv_sem=yrecv.at[src],
            device_id=(e, zb), device_id_type=MESH,
        )

    def part(delta):
        zb = zz(delta)
        for copy in ar[wide_far, delta]:
            copy.wait_recv()
        value = dot_nt(gd, W[1, zb].reshape(512, 384)) + dot_nt(ud, W[2, zb].reshape(512, 384))

        @pl.when(lax.rem(zb, 2) == c)
        def _():
            K[zb] = value

        @pl.when(lax.rem(zb, 2) != c)
        def _():
            XS[zb] = value.astype(BF16)
            sib_copy(zb).start()

    def pass_on(delta):
        zb = zz(delta)

        @pl.when(lax.rem(zb, 2) == c)
        def _():
            sib_copy(zb).wait_recv()
            K[zb] = K[zb] + XR[zb].astype(F32)

            @pl.when(zb != t)
            def _():
                YS[zb] = K[zb].astype(BF16)
                y_copy(zb, yl).start()

    part(0)
    part(-1)
    pass_on(0)
    part(1)
    pass_on(-1)
    pass_on(1)
    part(-2)
    part(2)
    pass_on(-2)
    pass_on(2)
    for copy in ret2:
        copy.wait_recv()
    back = RT2[...].reshape(64, 128)
    jf = (j * CAP).astype(F32)
    for k in range(2):
        scores = jnp.dot(
            onehot[k][:, 0:64], back, preferred_element_type=F32, precision=lax.Precision.HIGHEST
        )
        score = jnp.sum(jnp.where(lane == rank[k] + jf, scores, 0.0), axis=1, keepdims=True)
        out_r[k : k + 1, :] = jnp.sum(jnp.where(lane == row, score, 0.0), axis=0, keepdims=True)

    part(-3)
    part(3)
    pass_on(-3)
    b_step(4)
    pass_on(3)
    part(4)
    pass_on(4)
    total = K[t]
    for d in range(1, 4):
        src = lax.rem(yl + d, 4)
        y_copy(t, src).wait_recv()
        total += YR[src].astype(F32)
    out_g[...] = total.astype(BF16)
    for d in range(1, 4):
        y_copy(lax.rem(yl + d, 4) * 2 + c, yl).wait_send()
    for q in range(4):
        sib_copy(q * 2 + 1 - c).wait_send()
    for copy in sends:
        copy.wait_send()


def body(
    grad_out, dense_gate, dense_up, w_gate, w_up, w_down, routes, route_weight,
    expert_down, expert_hidden,
):
    p2, p3, p4, p5, m5 = tables()
    vmem = pl.BlockSpec(memory_space=pltpu.VMEM)
    hbm = pl.BlockSpec(memory_space=pltpu.HBM)
    out_g, out_h, out_r = pl.pallas_call(
        kernel,
        out_shape=(
            jax.ShapeDtypeStruct((128, 512), BF16),
            jax.ShapeDtypeStruct((320, 384), BF16),
            jax.ShapeDtypeStruct((2, 128), F32),
        ),
        in_specs=[vmem] + [hbm] * 14,
        out_specs=(vmem, vmem, vmem),
        scratch_shapes=[
            pltpu.VMEM((128, 384), BF16),
            pltpu.VMEM((128, 384), BF16),
            pltpu.VMEM((2, 128), jnp.int32),
            pltpu.VMEM((320, 384), BF16),
            pltpu.VMEM((8 * BLK, 8 * BLK), BF16),
            pltpu.VMEM((320, 8 * BLK), BF16),
            pltpu.VMEM((64, 8 * BLK), BF16),
            pltpu.VMEM((320, 128), BF16),
            pltpu.VMEM((320, 128), F32),
            pltpu.VMEM((3, 8, 2, 4, 64, 384), BF16),
            pltpu.VMEM((8, 128, 512), BF16),
            pltpu.VMEM((2, 8, 160, 512), BF16),
            pltpu.VMEM((8, BLK, 512), BF16),
            pltpu.VMEM((8, BLK, 512), BF16),
            pltpu.VMEM((4, 96, 512), BF16),
            pltpu.VMEM((4, 96, 512), BF16),
            pltpu.VMEM((2, 160, 512), BF16),
            pltpu.VMEM((2, 32, 128), BF16),
            pltpu.VMEM((32, 128), BF16),
            pltpu.VMEM((384, 4096), BF16),
            pltpu.VMEM((2, 160, 384), F32),
            pltpu.VMEM((320, 384), F32),
            pltpu.VMEM((8, 128, 512), F32),
            pltpu.VMEM((8, 128, 512), BF16),
            pltpu.VMEM((8, 128, 512), BF16),
            pltpu.VMEM((8, 128, 512), BF16),
            pltpu.VMEM((4, 128, 512), BF16),
            pltpu.VMEM((8, 8, 128), F32),
            pltpu.VMEM((8, 8, 128), F32),
            pltpu.VMEM((8, 8, 128), F32),
            pltpu.VMEM((8, 8, 128), F32),
            pltpu.SemaphoreType.DMA((N_COPY,)),
            pltpu.SemaphoreType.DMA((N_COPY,)),
            pltpu.SemaphoreType.DMA((16,)),
            pltpu.SemaphoreType.DMA((8,)),
            pltpu.SemaphoreType.DMA((8,)),
            pltpu.SemaphoreType.DMA((8,)),
            pltpu.SemaphoreType.DMA((4,)),
        ],
        compiler_params=pltpu.CompilerParams(
            collective_id=0, has_side_effects=True, vmem_limit_bytes=60 << 20
        ),
    )(
        route_weight.T, grad_out, dense_gate, dense_up, w_down.T, w_gate, w_up, routes.T,
        expert_down[0], expert_hidden[0],
        jnp.asarray(p2, BF16), jnp.asarray(p3, BF16), jnp.asarray(p4, BF16), jnp.asarray(p5, BF16),
        jnp.asarray(m5, F32),
    )
    return out_g, out_h[None], out_r.T


def solution(mesh):
    in_specs = (
        P("expert", "tensor"),
        P("expert", "tensor"),
        P("expert", "tensor"),
        P("expert", "tensor"),
        P("expert", "tensor"),
        P("tensor", "expert"),
        P("expert", None),
        P("expert", None),
        P("expert", "tensor", None),
        P("expert", None, "tensor"),
    )
    out_specs = (P("expert", "tensor"), P("expert", None, "tensor"), P("expert", None))
    return jax.shard_map(body, mesh=mesh, in_specs=in_specs, out_specs=out_specs, check_vma=False)
```
